128 devices in a mesh: panel: 4 (over z), front: 32 (over x, y, core).
Axes of the slice: x: 4, y: 4, z: 4, core: 2. Of those that a mesh axis runs over, the one named last changes fastest.
Arguments:
- source: float32 [2, 24, 32, 256, 512], P(None, None, 'panel', 'front'), may hold values from -6 to 6
- wave_term: float32 [32, 256, 512], P('panel', 'front'), may hold values from 0.5 to 2.5
- leaf_inverse: bfloat16 [2, 4, 32, 512, 512], P(None, 'panel', 'front'), may hold values from -0.1875 to 0.1875
- separator_inverse: bfloat16 [2, 4, 32, 4, 512, 512], P(None, 'panel', 'front'), may hold values from -0.1875 to 0.1875
- restrict_weight: float32 [32, 256], P('panel', 'front'), may hold values from 0.01 to 0.1
- prolong_weight: float32 [32, 256], P('panel', 'front'), may hold values from 0.05 to 0.5
Outputs:
- solution: float32 [2, 24, 32, 256, 512], P(None, None, 'panel', 'front')
- residual: float32 [2, 24, 32, 256, 512], P(None, None, 'panel', 'front')
The draws below stay inside these ranges and needn't reach their ends.
All inputs are finite; a program needn't handle non-finite values.
Results may differ from the reference program's by a relative error of at most 0.0055.
Values may be sent and summed in bfloat16 or wider, within the bound.
No kernel may reach another device: no remote copies, remote signals or barrier semaphores. Data moves between devices by JAX's collectives and lax.ppermute only.
A program may use at most 128 MiB of HBM per device.

```python
import math
import jax
import jax.numpy as jnp
from jax import lax

SOURCES = 24
PLANES = 8
ROWS = 8
NY = 512
LEVELS = 4
PANELS = 4
FRONTS = 32
NZ = 32
NX = 256


def block_levels(stream_key, extent, shards, smallest, high):
    factor_of = 1.0
    for position, shards_of in shards:
        heights = jax.random.uniform(jax.random.fold_in(jax.random.fold_in(stream_key, 6), position), (shards_of,), jnp.float32, smallest / len(shards), high / len(shards))
        factor_of = factor_of * jnp.repeat(jnp.exp(heights), extent[position] // shards_of).reshape((-1,) + (1,) * (len(extent) - 1 - position))
    return factor_of


def bell_draw(own_key, dims, scale, most, pieces=(), kind=jnp.bfloat16):
    drawn = jax.random.normal(own_key, dims, jnp.float32) * scale
    if len(pieces) > 0:
        drawn = block_levels(own_key, dims, pieces, -0.22, 0.18) * drawn
    return jnp.clip(drawn, min=-most, max=most).astype(kind)


def setup_inputs(seed: int = 0) -> dict:
    arg_keys = jax.random.split(jax.random.key(seed), 7)
    source = bell_draw(arg_keys[0], (2, SOURCES, NZ, NX, NY), 1.0, 6.0, ((2, 4), (3, 32)), jnp.float32)
    wave_term = jnp.clip(0.5 + 2.0 * jax.random.uniform(arg_keys[1], (NZ, NX, NY), jnp.float32) ** block_levels(arg_keys[1], (NZ, NX, NY), ((0, 4), (1, 32)), -0.2, 0.2), 0.5, 2.5)
    leaf_inverse = bell_draw(arg_keys[2], (2, PANELS, FRONTS, NY, NY), (2 * NY) ** -0.5, 0.1875, ((1, 4), (2, 32)))
    separator_inverse = bell_draw(arg_keys[3], (2, PANELS, FRONTS, LEVELS, NY, NY), (2 * NY) ** -0.5, 0.1875, ((1, 4), (2, 32)))
    restrict_weight = jnp.clip(jnp.exp(math.log(0.1) - 2.3025851 * jax.random.uniform(arg_keys[4], (NZ, NX), jnp.float32) ** block_levels(arg_keys[4], (NZ, NX), ((0, 4), (1, 32)), -0.2, 0.2)), 0.01, 0.1)
    prolong_weight = jnp.clip(jnp.exp(math.log(0.5) - 2.3025851 * jax.random.uniform(arg_keys[5], (NZ, NX), jnp.float32) ** block_levels(arg_keys[5], (NZ, NX), ((0, 4), (1, 32)), -0.2, 0.2)), 0.05, 0.5)
    return {"source": source, "wave_term": wave_term, "leaf_inverse": leaf_inverse, "separator_inverse": separator_inverse, "restrict_weight": restrict_weight, "prolong_weight": prolong_weight}


DAMPING = 0.25


def complex_block(inverse):
    top_half = jnp.concatenate([inverse[0], inverse[1]], axis=1)
    low_half = jnp.concatenate([-inverse[1], inverse[0]], axis=1)
    return jnp.concatenate([top_half, low_half], axis=0)


def reference(source, wave_term, leaf_inverse, separator_inverse, restrict_weight, prolong_weight):
    source_lines = jnp.concatenate([source[0], source[1]], axis=-1)

    def leaf_solve(panel_rhs, panel_no):
        plane_count = panel_rhs.shape[1]
        blocks = jax.vmap(complex_block, in_axes=1)(leaf_inverse[:, panel_no]).astype(jnp.float32)
        rounded = lax.optimization_barrier(panel_rhs.astype(jnp.bfloat16))
        shaped = rounded.astype(jnp.float32).reshape(SOURCES, plane_count, FRONTS, ROWS, 2 * NY)
        return jnp.einsum("bzfrk,fkv->bzfrv", shaped, blocks, precision=lax.Precision.HIGHEST)

    def correction(leaf_out, weights, panel_no):
        plane_count = leaf_out.shape[1]
        shaped_weights = weights.reshape(plane_count, FRONTS, ROWS)
        partial_value = jnp.einsum("bzfrv,zfr->fbv", leaf_out, shaped_weights, precision=lax.Precision.HIGHEST)
        level_sums = []
        for depth in range(1, 4):
            group_size = 2 ** depth
            summed = partial_value.reshape(FRONTS // group_size, group_size, SOURCES, 2 * NY).sum(axis=1)
            level_sums.append(jnp.repeat(summed, group_size, axis=0))
        level_sums.append(jnp.broadcast_to(partial_value.sum(axis=0), partial_value.shape))
        stacked = lax.optimization_barrier(jnp.stack(level_sums, axis=1).astype(jnp.bfloat16))
        blocks = jax.vmap(jax.vmap(complex_block, in_axes=1), in_axes=1)(separator_inverse[:, panel_no])
        return jnp.einsum("flbk,flkv->fbv", stacked.astype(jnp.float32), blocks.astype(jnp.float32),
                          precision=lax.Precision.HIGHEST)

    def spread(correction_now, weights):
        shaped_weights = weights.reshape(PLANES, FRONTS, ROWS)
        moved = jnp.transpose(correction_now, (1, 0, 2))
        spread_out = shaped_weights[None, :, :, :, None] * moved[:, None, :, None, :]
        return spread_out.reshape(SOURCES, PLANES, NX, 2 * NY)

    forward_list = []
    previous = None
    for panel_no in range(PANELS):
        start = panel_no * PLANES
        panel_rhs = source_lines[:, start:start + PLANES]
        leaf_out = leaf_solve(panel_rhs, panel_no)
        correction_now = correction(leaf_out, restrict_weight[start:start + PLANES], panel_no)
        result = leaf_out.reshape(SOURCES, PLANES, NX, 2 * NY) + spread(correction_now, prolong_weight[start:start + PLANES])
        if previous is not None:
            leaf_one = leaf_solve(previous[:, None], panel_no)
            corr_one = correction(leaf_one, restrict_weight[start:start + 1], panel_no)
            update = spread(corr_one, prolong_weight[start:start + PLANES])
            first_plane = update[:, :1] + leaf_one.reshape(SOURCES, 1, NX, 2 * NY)
            result = result + jnp.concatenate([first_plane, update[:, 1:]], axis=1)
        forward_list.append(result)
        previous = result[:, -1]

    swept_list = list(forward_list)
    for panel_no in range(PANELS - 2, -1, -1):
        start = panel_no * PLANES
        arriving = swept_list[panel_no + 1][:, 0]
        leaf_out = leaf_solve(arriving[:, None], panel_no)
        correction_now = correction(leaf_out, restrict_weight[start + PLANES - 1:start + PLANES], panel_no)
        update = spread(correction_now, prolong_weight[start:start + PLANES])
        last_plane = update[:, -1:] + leaf_out.reshape(SOURCES, 1, NX, 2 * NY)
        swept_list[panel_no] = forward_list[panel_no] + jnp.concatenate([update[:, :-1], last_plane], axis=1)

    whole_lines = jnp.concatenate(swept_list, axis=1)
    wavefield = jnp.stack([whole_lines[..., :NY], whole_lines[..., NY:]])
    padded = jnp.pad(wavefield, ((0, 0), (0, 0), (1, 1), (1, 1), (1, 1)))
    neighbours = padded[:, :, 2:, 1:-1, 1:-1] + padded[:, :, :-2, 1:-1, 1:-1]
    neighbours = neighbours + padded[:, :, 1:-1, 2:, 1:-1] + padded[:, :, 1:-1, :-2, 1:-1]
    neighbours = neighbours + padded[:, :, 1:-1, 1:-1, 2:] + padded[:, :, 1:-1, 1:-1, :-2]
    diag_real = 6.0 - wave_term
    diag_imag = -DAMPING * wave_term
    applied_real = diag_real * wavefield[0] - diag_imag * wavefield[1] - neighbours[0]
    applied_imag = diag_real * wavefield[1] + diag_imag * wavefield[0] - neighbours[1]
    residual = jnp.stack([source[0] - applied_real, source[1] - applied_imag])
    return wavefield, residual
```

```python
import jax
import jax.numpy as jnp
from jax import lax
from jax.experimental import pallas as pl
from jax.experimental.pallas import tpu as pltpu
from jax.sharding import PartitionSpec as P

DAMPING = 0.25
PANELS = 4
FRONTS = 32
AXES = ("panel", "front")
BF = jnp.bfloat16
F32 = jnp.float32
PAIRS = {"A": ((0, 1), (2, 3)), "B": ((1, 2), (0, 3))}


def pairing(swaps):
    target = {}
    for one, two in swaps:
        target[one] = two
        target[two] = one
    for device in range(PANELS * FRONTS):
        target.setdefault(device, device ^ 1)
    return sorted(target.items())


def within(panels, even, odd):
    swaps = []
    for panel in panels:
        for front in range(FRONTS):
            other = front ^ (odd if front % 2 else even)
            swaps.append((panel * FRONTS + front, panel * FRONTS + other))
    return pairing(swaps)


def across(pairs, even, odd):
    swaps = []
    for one, two in pairs:
        for front in range(FRONTS):
            other = front ^ (odd if front % 2 else even)
            swaps.append((one * FRONTS + front, two * FRONTS + other))
    return pairing(swaps)


def moved(block, route):
    return lax.ppermute(block, AXES, route)


def other_core(block):
    return moved(block, pairing(()))


def swapped(block, which):
    return moved(block, across(PAIRS[which], 0, 0))


def leaf_kernel(source_ref, matrix_ref, weight_ref, leaf_ref, total_ref, first_ref, last_ref):
    count, planes, rows, width = source_ref.shape[1:]
    flat = count * planes * rows
    real = source_ref[0].reshape(flat, width).astype(BF)
    imag = source_ref[1].reshape(flat, width).astype(BF)
    dot = lambda a, b: jnp.dot(a, b, preferred_element_type=F32)
    out = (
        dot(real, matrix_ref[0]) - dot(imag, matrix_ref[1]),
        dot(real, matrix_ref[1]) + dot(imag, matrix_ref[0]),
    )
    for part in range(2):
        shaped = out[part].reshape(count, planes, rows, width)
        leaf_ref[part] = shaped
        first_ref[part] = shaped[:, 0].astype(BF)
        last_ref[part] = shaped[:, planes - 1].astype(BF)
        total_ref[0, part] = jnp.sum(shaped * weight_ref[...][None], axis=(1, 2))


def leaf_solve(source, matrix, weights):
    two, sources, planes, rows, width = source.shape
    step = 4
    whole = pl.BlockSpec((two, step, planes, rows, width), lambda i: (0, i, 0, 0, 0))
    plane = pl.BlockSpec((two, step, rows, width), lambda i: (0, i, 0, 0))
    leaf, total, first, last = pl.pallas_call(
        leaf_kernel,
        grid=(sources // step,),
        in_specs=[
            whole,
            pl.BlockSpec((two, width, width), lambda i: (0, 0, 0)),
            pl.BlockSpec((planes, rows, width), lambda i: (0, 0, 0)),
        ],
        out_specs=[whole, pl.BlockSpec((1, two, step, width), lambda i: (i, 0, 0, 0)), plane, plane],
        out_shape=[
            jax.ShapeDtypeStruct(source.shape, F32),
            jax.ShapeDtypeStruct((sources // step, two, step, width), F32),
            jax.ShapeDtypeStruct((two, sources, rows, width), BF),
            jax.ShapeDtypeStruct((two, sources, rows, width), BF),
        ],
        compiler_params=pltpu.CompilerParams(vmem_limit_bytes=40 * 2**20),
        cost_estimate=pl.CostEstimate(flops=6500000000, bytes_accessed=16000000, transcendentals=0),
        name="leaf_solve",
    )(source, matrix, weights)
    return leaf, total.transpose(1, 0, 2, 3).reshape(two, sources, width), first, last


def final_kernel(
    leaf_ref, source_ref, wave_ref, prolong_ref, vector_ref, first_ref, last_ref,
    xlow_ref, xhigh_ref, zlow_ref, zhigh_ref, field_ref, residual_ref,
):
    count, planes, rows, width = leaf_ref.shape[1:]
    column = lax.broadcasted_iota(jnp.int32, (rows, width), 1)
    row = lax.broadcasted_iota(jnp.int32, (rows, width), 0)
    for b in range(count):
        field = []
        for part in range(2):
            vector = vector_ref[part, b]
            tiles = []
            for z in range(planes):
                tile = leaf_ref[part, b, z] + prolong_ref[z] * vector
                if z == 0:
                    tile = tile + first_ref[part, b]
                if z == planes - 1:
                    tile = tile + last_ref[part, b]
                field_ref[part, b, z] = tile
                tiles.append(tile)
            field.append(tiles)
        for z in range(planes):
            diag_real = 6.0 - wave_ref[z]
            diag_imag = -DAMPING * wave_ref[z]
            for part in range(2):
                tiles = field[part]
                here = tiles[z]
                below = tiles[z - 1] if z else zlow_ref[part, b].astype(F32)
                above = tiles[z + 1] if z < planes - 1 else zhigh_ref[part, b].astype(F32)
                near = below + above
                low = jnp.where(row == 0, xlow_ref[part, b, z].astype(F32)[None], pltpu.roll(here, 1, 0))
                high = jnp.where(row == rows - 1, xhigh_ref[part, b, z].astype(F32)[None], pltpu.roll(here, rows - 1, 0))
                near = near + low + high
                left = jnp.where(column == 0, 0.0, pltpu.roll(here, 1, 1))
                right = jnp.where(column == width - 1, 0.0, pltpu.roll(here, width - 1, 1))
                near = near + left + right
                cross = diag_imag * field[1 - part][z]
                applied = diag_real * here - near
                applied = applied - cross if part == 0 else applied + cross
                residual_ref[part, b, z] = source_ref[part, b, z] - applied


def finish(leaf, source, wave_term, prolong, vector, first, last, xlow, xhigh, zlow, zhigh):
    two, sources, planes, rows, width = source.shape
    step = 2
    whole = pl.BlockSpec((two, step, planes, rows, width), lambda i: (0, i, 0, 0, 0))
    plane = pl.BlockSpec((two, step, rows, width), lambda i: (0, i, 0, 0))
    fixed = pl.BlockSpec((planes, rows, width), lambda i: (0, 0, 0))
    return pl.pallas_call(
        final_kernel,
        grid=(sources // step,),
        in_specs=[
            whole, whole, fixed, fixed,
            pl.BlockSpec((two, step, 1, width), lambda i: (0, i, 0, 0)),
            plane, plane, plane, plane, plane, plane,
        ],
        out_specs=[whole, whole],
        out_shape=[jax.ShapeDtypeStruct(source.shape, F32)] * 2,
        compiler_params=pltpu.CompilerParams(vmem_limit_bytes=40 * 2**20),
        cost_estimate=pl.CostEstimate(flops=60000000, bytes_accessed=26000000, transcendentals=0),
        name="finish",
    )(leaf, source, wave_term, prolong, vector[:, :, None], first, last, xlow, xhigh, zlow, zhigh)


def times(block, matrix):
    shape = block.shape[1:-1]
    flat = block.astype(BF).reshape(-1, block.shape[-1])
    half = flat.shape[0] // 2
    by_real = jnp.dot(flat, matrix[0], preferred_element_type=F32)
    by_imag = jnp.dot(flat, matrix[1], preferred_element_type=F32)
    out = jnp.stack([by_real[:half] - by_imag[half:], by_imag[:half] + by_real[half:]])
    return out.reshape((2,) + shape + (matrix.shape[-1],))


def local(source, wave_term, leaf_inverse, separator_inverse, restrict_weight, prolong_weight):
    two, sources, planes, rows, width = source.shape
    panel = lax.axis_index("panel")
    front = lax.axis_index("front")
    even_core = front % 2 == 0
    even_panel = panel % 2 == 0
    leaf_matrix = leaf_inverse[:, 0, 0]
    separators = separator_inverse[:, 0, 0]
    near_matrix = separators[:, :3].reshape(2, 3 * width, width)
    root_matrix = separators[:, 3]

    weights = jnp.stack([restrict_weight, prolong_weight])
    traded_weights = {which: swapped(weights, which) for which in "AB"}
    traded_leaf = {which: swapped(leaf_matrix, which) for which in "AB"}

    wide = lambda table: jnp.broadcast_to(table[:, :, None], table.shape + (width,))
    leaf, base_terms, first_plane, last_plane = leaf_solve(source, leaf_matrix, wide(restrict_weight))

    def halves(block):
        return jnp.where(even_core, block[0], block[1])

    def joined(mine, other):
        return jnp.where(even_core, jnp.stack([mine, other]), jnp.stack([other, mine]))

    def inside(block, panels, near, far, cross):
        sent = block.astype(BF)
        side = moved(sent, within(panels, near, cross))
        opposite = moved(halves(sent), within(panels, far, far))
        got = jnp.concatenate([side, opposite[None]])
        back = other_core(got)
        near_term = jnp.where(even_core, side, back[:2]).astype(F32)
        total = side.astype(F32) + back[:2].astype(F32) + joined(opposite, back[2]).astype(F32)
        return near_term, total

    def root_sum(slab, panels):
        return slab + inside(slab, panels, 8, 16, 24)[1]

    def corrected(near_sums, slab, panels):
        stacked = jnp.concatenate([term.astype(BF) for term in near_sums], axis=-1)
        partial_value = times(stacked, near_matrix)
        return partial_value + times(root_sum(slab, panels), root_matrix)

    def first_correction(terms):
        pair = terms + other_core(terms.astype(BF)).astype(F32)
        near_term, total = inside(pair, (0,), 2, 4, 6)
        slab = pair + total
        return corrected((pair, pair + near_term, slab), slab, (0,))

    def step_correction(terms, from_panel, to_panel):
        pair = (terms + other_core(terms.astype(BF)).astype(F32)).astype(BF)
        ends = ((from_panel, to_panel),)
        one = moved(pair, across(ends, 0, 2))
        two_ = moved(pair, across(ends, 4, 6))
        back = other_core(jnp.stack([one, two_])).astype(F32)
        one = one.astype(F32)
        own = jnp.where(even_core, one, back[0])
        quad = one + back[0]
        slab = quad + two_.astype(F32) + back[1]
        return corrected((own, quad, slab), slab, (to_panel,))

    def weighted(row_weights, plane):
        return jnp.einsum("cbxv,x->cbv", plane.astype(F32), row_weights, precision=lax.Precision.HIGHEST)

    below = jnp.where(even_panel, swapped(last_plane, "B"), swapped(last_plane, "A"))
    below = jnp.where(panel > 0, below, 0)
    entering = times(below, leaf_matrix)
    first_whole = (first_plane.astype(F32) + entering).astype(BF)
    above = jnp.where(even_panel, swapped(first_whole, "A"), swapped(first_whole, "B"))
    above = jnp.where(panel < PANELS - 1, above, 0)
    leaving = times(above, leaf_matrix)

    traded_terms = {which: swapped(base_terms.astype(BF), which).astype(F32) for which in "AB"}
    correction = first_correction(base_terms)
    entered = jnp.zeros_like(correction)
    left_behind = jnp.zeros_like(correction)
    for turn, which in enumerate("ABA"):
        target = turn + 1
        row_weights = traded_weights[which][0, 0]
        start = weighted(row_weights, last_plane) + jnp.sum(row_weights * prolong_weight[-1]) * correction
        start = jnp.concatenate([start, correction], axis=1)
        product = times(start, traded_leaf[which])
        terms = product[:, :sources] + traded_terms[which]
        carried = product[:, sources:]
        left_behind = jnp.where(panel == turn, carried, left_behind)
        entered = jnp.where(panel == target, swapped(carried.astype(BF), which).astype(F32), entered)
        correction = jnp.where(panel == target, step_correction(terms, turn, target), correction)
    for turn, which in enumerate("ABA"):
        from_panel = PANELS - 1 - turn
        target = from_panel - 1
        row_weights = traded_weights[which][0, -1]
        start = weighted(row_weights, first_whole)
        start = start + jnp.sum(row_weights * prolong_weight[0]) * correction
        start = start + jnp.sum(row_weights * traded_weights[which][1, -1]) * entered
        terms = times(start, traded_leaf[which])
        correction = correction + jnp.where(panel == target, step_correction(terms, from_panel, target), 0)

    upper = jnp.where(even_panel, swapped(correction, "A"), swapped(correction, "B"))
    upper = jnp.where(panel < PANELS - 1, upper, 0)
    upper_weights = jnp.where(even_panel, traded_weights["A"], traded_weights["B"])
    lower_weights = jnp.where(even_panel, traded_weights["B"], traded_weights["A"])
    outgoing = times(jnp.concatenate([upper, left_behind], axis=1), leaf_matrix)
    spread = lambda row_weights, vector: row_weights[:, None] * vector[:, :, None, :]
    first_add = entering + jnp.where(panel > 0, spread(lower_weights[1, -1], entered), 0)
    last_add = leaving + spread(upper_weights[1, 0], outgoing[:, :sources])
    last_add = last_add + spread(prolong_weight[-1], outgoing[:, sources:])
    last_add = jnp.where(panel < PANELS - 1, last_add, 0)

    def edge_row(x):
        edge = leaf[:, :, :, x] + spread(prolong_weight[:, x], correction)
        edge = edge.at[:, :, 0].add(first_add[:, :, x]).at[:, :, -1].add(last_add[:, :, x])
        return edge.astype(BF)

    low_edge, high_edge = edge_row(0), edge_row(rows - 1)
    near_front = other_core(jnp.where(even_core, high_edge, low_edge))
    chain = [(p * FRONTS + f, p * FRONTS + (f + 1) % FRONTS) for p in range(PANELS) for f in range(1, FRONTS, 2)]
    far_front = moved(jnp.where(even_core, low_edge, high_edge), pairing(chain))
    xlow = jnp.where(even_core, jnp.where(front > 0, far_front, 0), near_front)
    xhigh = jnp.where(even_core, near_front, jnp.where(front < FRONTS - 1, far_front, 0))
    low_plane = (leaf[:, :, 0] + spread(prolong_weight[0], correction) + first_add).astype(BF)
    high_plane = (leaf[:, :, -1] + spread(prolong_weight[-1], correction) + last_add).astype(BF)
    by_a = swapped(jnp.where(even_panel, high_plane, low_plane), "A")
    by_b = swapped(jnp.where(even_panel, low_plane, high_plane), "B")
    zlow = jnp.where(panel > 0, jnp.where(even_panel, by_b, by_a), 0)
    zhigh = jnp.where(panel < PANELS - 1, jnp.where(even_panel, by_a, by_b), 0)
    return tuple(
        finish(
            leaf, source, wave_term, wide(prolong_weight), correction, first_add, last_add,
            xlow, xhigh, zlow, zhigh,
        )
    )


def solution(mesh):
    placed = (
        P(None, None, "panel", "front", None),
        P("panel", "front", None),
        P(None, "panel", "front", None, None),
        P(None, "panel", "front", None, None, None),
        P("panel", "front"),
        P("panel", "front"),
    )
    return jax.shard_map(
        local,
        mesh=mesh,
        in_specs=placed,
        out_specs=(P(None, None, "panel", "front", None), P(None, None, "panel", "front", None)),
        check_vma=False,
    )
```

```python
import jax
import jax.numpy as jnp
from jax import lax
from jax.experimental import pallas as pl
from jax.experimental.pallas import tpu as pltpu
from jax.sharding import PartitionSpec as P

DAMPING = 0.25
PANELS = 4
FRONTS = 32
AXES = ("panel", "front")
BF = jnp.bfloat16
F32 = jnp.float32
PAIRS = {"A": ((0, 1), (2, 3)), "B": ((1, 2), (0, 3))}


def pairing(swaps):
    target = {}
    for one, two in swaps:
        target[one] = two
        target[two] = one
    for device in range(PANELS * FRONTS):
        target.setdefault(device, device ^ 1)
    return sorted(target.items())


def within(panels, even, odd):
    swaps = []
    for panel in panels:
        for front in range(FRONTS):
            other = front ^ (odd if front % 2 else even)
            swaps.append((panel * FRONTS + front, panel * FRONTS + other))
    return pairing(swaps)


def across(pairs, even, odd):
    swaps = []
    for one, two in pairs:
        for front in range(FRONTS):
            other = front ^ (odd if front % 2 else even)
            swaps.append((one * FRONTS + front, two * FRONTS + other))
    return pairing(swaps)


def moved(block, route):
    return lax.ppermute(block, AXES, route)


def other_core(block):
    return moved(block, pairing(()))


def swapped(block, which):
    return moved(block, across(PAIRS[which], 0, 0))


def product(block, matrix_real, matrix_imag, half):
    by_real = jnp.dot(block, matrix_real, preferred_element_type=F32)
    by_imag = jnp.dot(block, matrix_imag, preferred_element_type=F32)
    return by_real[:half] - by_imag[half:], by_imag[:half] + by_real[half:]


def leaf_kernel(source_ref, matrix_ref, weight_ref, leaf_ref, total_ref, first_ref, last_ref, low_ref, high_ref):
    count, planes, rows, width = source_ref.shape[1:]
    flat = count * planes * rows
    real = source_ref[0].reshape(flat, width).astype(BF)
    imag = source_ref[1].reshape(flat, width).astype(BF)
    dot = lambda a, b: jnp.dot(a, b, preferred_element_type=F32)
    out = (
        dot(real, matrix_ref[0]) - dot(imag, matrix_ref[1]),
        dot(real, matrix_ref[1]) + dot(imag, matrix_ref[0]),
    )
    for part in range(2):
        shaped = out[part].reshape(count, planes, rows, width)
        leaf_ref[part] = shaped
        first_ref[part] = shaped[:, 0].astype(BF)
        last_ref[part] = shaped[:, planes - 1].astype(BF)
        low_ref[part] = shaped[:, :, 0]
        high_ref[part] = shaped[:, :, rows - 1]
        total_ref[0, part] = jnp.sum(shaped * weight_ref[...][None], axis=(1, 2))


def leaf_solve(source, matrix, weights):
    two, sources, planes, rows, width = source.shape
    step = 4
    whole = pl.BlockSpec((two, step, planes, rows, width), lambda i: (0, i, 0, 0, 0))
    plane = pl.BlockSpec((two, step, rows, width), lambda i: (0, i, 0, 0))
    leaf, total, first, last, low, high = pl.pallas_call(
        leaf_kernel,
        grid=(sources // step,),
        in_specs=[
            whole,
            pl.BlockSpec((two, width, width), lambda i: (0, 0, 0)),
            pl.BlockSpec((planes, rows, width), lambda i: (0, 0, 0)),
        ],
        out_specs=[whole, pl.BlockSpec((1, two, step, width), lambda i: (i, 0, 0, 0)), plane, plane, plane, plane],
        out_shape=[
            jax.ShapeDtypeStruct(source.shape, F32),
            jax.ShapeDtypeStruct((sources // step, two, step, width), F32),
            jax.ShapeDtypeStruct((two, sources, rows, width), BF),
            jax.ShapeDtypeStruct((two, sources, rows, width), BF),
            jax.ShapeDtypeStruct((two, sources, planes, width), F32),
            jax.ShapeDtypeStruct((two, sources, planes, width), F32),
        ],
        compiler_params=pltpu.CompilerParams(vmem_limit_bytes=24 * 2**20),
        cost_estimate=pl.CostEstimate(flops=65000000, bytes_accessed=1600000, transcendentals=0),
        name="leaf_solve",
    )(source, matrix, weights)
    return leaf, total.transpose(1, 0, 2, 3).reshape(two, sources, width), first, last, low, high


def whole_call(kernel, shapes, cost, name, smem, *args):
    spaces = [pltpu.SMEM] * smem + [pltpu.VMEM] * (len(args) - smem)
    return pl.pallas_call(
        kernel,
        in_specs=[pl.BlockSpec(memory_space=space) for space in spaces],
        out_specs=[pl.BlockSpec(memory_space=pltpu.VMEM)] * len(shapes),
        out_shape=shapes,
        compiler_params=pltpu.CompilerParams(vmem_limit_bytes=16 * 2**20),
        cost_estimate=pl.CostEstimate(flops=cost, bytes_accessed=cost // 200, transcendentals=0),
        name=name,
    )(*args)


def near_kernel(own_ref, quad_ref, slab_ref, matrix_ref, out_ref):
    sources, width = own_ref.shape[1:]
    total = None
    for level, ref in enumerate((own_ref, quad_ref, slab_ref)):
        block = ref[...].reshape(2 * sources, width).astype(BF)
        got = product(block, matrix_ref[0, level], matrix_ref[1, level], sources)
        total = got if total is None else (total[0] + got[0], total[1] + got[1])
    out_ref[0] = total[0]
    out_ref[1] = total[1]


def near_part(own, quad, slab, separators):
    return whole_call(
        near_kernel, [jax.ShapeDtypeStruct(own.shape, F32)], 150000000, "near_part", 0, own, quad, slab, separators
    )[0]


def advance_kernel(
    flag_ref, scale_ref, near_ref, slab_ref, side_ref, opposite_ref, back_ref, before_ref, base_ref,
    root_ref, top_ref, low_ref, state_ref, *out_refs,
):
    sources, width = near_ref.shape[1:]
    even = flag_ref[0] == 1
    active = flag_ref[1] == 1
    keep = flag_ref[2] == 1
    mine = opposite_ref[...].astype(F32)
    other = back_ref[2].astype(F32)
    root = []
    for part in range(2):
        far = jnp.where(even, mine, other) if part == 0 else jnp.where(even, other, mine)
        root.append(slab_ref[part] + side_ref[part].astype(F32) + back_ref[part].astype(F32) + far)
    block = jnp.concatenate(root, axis=0).astype(BF)
    got = product(block, root_ref[0], root_ref[1], sources)
    state = []
    for part in range(2):
        new = near_ref[part] + got[part]
        old = before_ref[part]
        state.append(jnp.where(active, new + jnp.where(keep, old, 0.0), old))
        state_ref[part] = state[part]
    count = base_ref.shape[0]
    rows = [base_ref[i, part] + scale_ref[i] * state[part] for part in range(2) for i in range(count)]
    block = jnp.concatenate(rows, axis=0).astype(BF)
    half = width // 2
    one = product(block[:, :half], top_ref[0], top_ref[1], count * sources)
    two = product(block[:, half:], low_ref[0], low_ref[1], count * sources)
    for part in range(2):
        out = (one[part] + two[part]).astype(BF)
        for i in range(count):
            out_refs[i][part] = out[i * sources : (i + 1) * sources]


def advance(flags, scales, near, slab, got, before, bases, root_matrix, halves):
    side, opposite, back = got
    vector = jax.ShapeDtypeStruct(near.shape, BF)
    out = whole_call(
        advance_kernel, [jax.ShapeDtypeStruct(near.shape, F32)] + [vector] * bases.shape[0], 200000000, "advance", 2,
        flags, scales, near, slab, side, opposite, back, before, bases, root_matrix, *halves,
    )
    return out


def sums_kernel(first_ref, last_ref, table_ref, out_ref):
    for part in range(2):
        last = last_ref[part].astype(F32)
        first = first_ref[part].astype(F32)
        for i in range(3):
            out_ref[i, part] = jnp.sum(last * table_ref[i][None], axis=1)
        for i in range(3, 5):
            out_ref[i, part] = jnp.sum(first * table_ref[i][None], axis=1)


def edge_sums(first, last, tables):
    two, sources, rows, width = first.shape
    shape = jax.ShapeDtypeStruct((5, two, sources, width), F32)
    return whole_call(sums_kernel, [shape], 10000000, "edge_sums", 0, first, last, tables)[0]


def edges_kernel(
    flag_ref, scale_ref, low_ref, high_ref, prolong_ref, vector_ref, enter_ref, leave_ref, near_ref, far_ref
):
    sources, planes, width = low_ref.shape[1:]
    rows = enter_ref.shape[2]
    even = flag_ref[0] == 1
    depth = lax.broadcasted_iota(jnp.int32, (planes, width), 0)
    for part in range(2):
        for b in range(sources):
            vec = vector_ref[part, b]
            done = []
            for side, ref in ((0, low_ref), (1, high_ref)):
                x = 0 if side == 0 else rows - 1
                enter = enter_ref[part, b, x : x + 1] + scale_ref[0, x] * vec[1:2]
                leave = leave_ref[part, b, x : x + 1] + scale_ref[1, x] * vec[5:6] + scale_ref[2, x] * vec[6:7]
                tile = ref[part, b] + prolong_ref[side] * vec[0:1]
                tile = tile + jnp.where(depth == 0, enter, 0.0) + jnp.where(depth == planes - 1, leave, 0.0)
                done.append(tile)
            near_ref[part, b] = jnp.where(even, done[1], done[0]).astype(BF)
            far_ref[part, b] = jnp.where(even, done[0], done[1]).astype(BF)


def edge_rows(flags, scales, low, high, prolong, vectors, enter, leave):
    shape = jax.ShapeDtypeStruct(low.shape, BF)
    return whole_call(
        edges_kernel, [shape, shape], 20000000, "edge_rows", 2, flags, scales, low, high, prolong, vectors, enter, leave
    )


def final_kernel(
    leaf_ref, source_ref, wave_ref, prolong_ref, table_ref, vector_ref, enter_ref, leave_ref,
    xlow_ref, xhigh_ref, zlow_ref, zhigh_ref, field_ref, residual_ref,
):
    count, planes, rows, width = leaf_ref.shape[1:]
    column = lax.broadcasted_iota(jnp.int32, (rows, width), 1)
    row = lax.broadcasted_iota(jnp.int32, (rows, width), 0)
    below_last, above_first = table_ref[0], table_ref[1]
    own_last, own_first = prolong_ref[planes - 1], prolong_ref[0]
    for b in range(count):
        field, ends = [], []
        for part in range(2):
            vec = [vector_ref[part, b, i : i + 1] for i in range(9)]
            tiles = []
            for z in range(planes):
                tile = leaf_ref[part, b, z] + prolong_ref[z] * vec[0]
                if z == 0:
                    tile = tile + enter_ref[part, b] + below_last * vec[1]
                if z == planes - 1:
                    tile = tile + leave_ref[part, b] + above_first * vec[5] + own_last * vec[6]
                field_ref[part, b, z] = tile
                tiles.append(tile)
            field.append(tiles)
            below = zlow_ref[part, b] + below_last * (vec[3] + vec[8]) + own_first * vec[7]
            above = zhigh_ref[part, b] + above_first * vec[2] + own_last * vec[4]
            ends.append((below, above))
        for z in range(planes):
            diag_real = 6.0 - wave_ref[z]
            diag_imag = -DAMPING * wave_ref[z]
            for part in range(2):
                tiles = field[part]
                here = tiles[z]
                below = tiles[z - 1] if z else ends[part][0]
                above = tiles[z + 1] if z < planes - 1 else ends[part][1]
                near = below + above
                low = jnp.where(row == 0, xlow_ref[part, b, z].astype(F32)[None], pltpu.roll(here, 1, 0))
                high = jnp.where(row == rows - 1, xhigh_ref[part, b, z].astype(F32)[None], pltpu.roll(here, rows - 1, 0))
                near = near + low + high
                left = jnp.where(column == 0, 0.0, pltpu.roll(here, 1, 1))
                right = jnp.where(column == width - 1, 0.0, pltpu.roll(here, width - 1, 1))
                near = near + left + right
                cross = diag_imag * field[1 - part][z]
                applied = diag_real * here - near
                applied = applied - cross if part == 0 else applied + cross
                residual_ref[part, b, z] = source_ref[part, b, z] - applied


def finish(leaf, source, wave_term, prolong, tables, vectors, enter, leave, xlow, xhigh, zlow, zhigh):
    two, sources, planes, rows, width = source.shape
    step = 2
    whole = pl.BlockSpec((two, step, planes, rows, width), lambda i: (0, i, 0, 0, 0))
    plane = pl.BlockSpec((two, step, rows, width), lambda i: (0, i, 0, 0))
    fixed = pl.BlockSpec((planes, rows, width), lambda i: (0, 0, 0))
    return pl.pallas_call(
        final_kernel,
        grid=(sources // step,),
        in_specs=[
            whole, whole, fixed, fixed,
            pl.BlockSpec((2, rows, width), lambda i: (0, 0, 0)),
            pl.BlockSpec((two, step, 9, width), lambda i: (0, i, 0, 0)),
            plane, plane, plane, plane, plane, plane,
        ],
        out_specs=[whole, whole],
        out_shape=[jax.ShapeDtypeStruct(source.shape, F32)] * 2,
        compiler_params=pltpu.CompilerParams(vmem_limit_bytes=24 * 2**20),
        cost_estimate=pl.CostEstimate(flops=60000000, bytes_accessed=26000000, transcendentals=0),
        name="finish",
    )(leaf, source, wave_term, prolong, tables, vectors, enter, leave, xlow, xhigh, zlow, zhigh)


def times(block, matrix):
    shape = block.shape[1:-1]
    flat = block.astype(BF).reshape(-1, block.shape[-1])
    half = flat.shape[0] // 2
    out = jnp.stack(product(flat, matrix[0], matrix[1], half))
    return out.reshape((2,) + shape + (matrix.shape[-1],))


def after(value, *others):
    return lax.optimization_barrier((value, *others))[0]


def local(source, wave_term, leaf_inverse, separator_inverse, restrict_weight, prolong_weight):
    two, sources, planes, rows, width = source.shape
    panel = lax.axis_index("panel")
    front = lax.axis_index("front")
    even_core = front % 2 == 0
    even_panel = panel % 2 == 0
    leaf_matrix = leaf_inverse[:, 0, 0]
    separators = separator_inverse[:, 0, 0]
    root_matrix = separators[:, 3]
    half = width // 2

    def by_parity(even_value, odd_value):
        return jnp.where(even_panel, even_value, odd_value)

    weights = jnp.stack([restrict_weight, prolong_weight])
    traded_weights = {which: swapped(weights, which) for which in "AB"}
    leaf_a = [swapped(leaf_matrix[:, :half], "A")]
    leaf_a.append(swapped(after(leaf_matrix[:, half:], leaf_a[0]), "A"))
    leaf_b = [swapped(after(leaf_matrix[:, :half], leaf_a[1]), "B")]
    leaf_b.append(swapped(after(leaf_matrix[:, half:], leaf_b[0]), "B"))
    traded_leaf = {"A": leaf_a, "B": leaf_b}

    wide = lambda table: jnp.broadcast_to(table[..., None], table.shape + (width,))
    leaf, base_terms, first_plane, last_plane, low_rows, high_rows = leaf_solve(
        source, leaf_matrix, wide(restrict_weight)
    )

    def halves(block):
        return jnp.where(even_core, block[0], block[1])

    def inside(sent, panels, near, far, cross):
        side = moved(sent, within(panels, near, cross))
        opposite = moved(halves(sent), within(panels, far, far))
        back = other_core(jnp.concatenate([side, opposite[None]]))
        return side, opposite, back

    def pair_sum(terms):
        return terms.astype(F32) + other_core(terms).astype(F32)

    every = tuple(range(PANELS))
    pair = pair_sum(base_terms.astype(BF))
    side, opposite, back = inside(pair.astype(BF), every, 2, 4, 6)
    near_term = jnp.where(even_core, side, back[:2]).astype(F32)
    far_term = jnp.where(even_core, jnp.stack([opposite, back[2]]), jnp.stack([back[2], opposite])).astype(F32)
    quad = pair + near_term
    slab = pair + side.astype(F32) + back[:2].astype(F32) + far_term
    base_sums = (pair, quad, slab)
    nothing = jnp.zeros((two, sources, width), F32)

    def flags(active, keep):
        return jnp.stack([even_core, active, jnp.full((), keep)]).astype(jnp.int32)

    def close(sums, panels, active, keep, before, bases, scales, which):
        own, quad, slab = sums
        got = inside(slab.astype(BF), panels, 8, 16, 24)
        near = near_part(own, quad, slab, separators)
        return advance(flags(active, keep), scales, near, slab, got, before, bases, root_matrix, traded_leaf[which])

    def cross(terms, from_panel, to_panel):
        sent = pair_sum(terms).astype(BF)
        ends = ((from_panel, to_panel),)
        one = moved(sent, across(ends, 0, 2))
        two_ = moved(sent, across(ends, 4, 6))
        back = other_core(jnp.stack([one, two_])).astype(F32)
        one = one.astype(F32)
        own = jnp.where(even_core, one, back[0])
        quad = one + back[0]
        return own, quad, quad + two_.astype(F32) + back[1]

    restrict = {which: traded_weights[which][0] for which in "AB"}
    prolong = {which: traded_weights[which][1] for which in "AB"}
    tables = jnp.stack(
        [restrict["A"][0], restrict["B"][0], restrict_weight[-1], restrict["A"][-1], restrict["B"][-1]]
    )
    sums = edge_sums(first_plane, last_plane, wide(tables))
    onward = {"A": sums[0], "B": sums[1]}
    returning = {"A": sums[3], "B": sums[4]}
    own_scale = jnp.sum(restrict_weight[-1] * prolong_weight[-1])

    def forward_bases(which):
        scale = jnp.sum(restrict[which][0] * prolong_weight[-1])
        return jnp.stack([onward[which], nothing, sums[2]]), jnp.stack([scale, jnp.ones((), F32), own_scale])

    def backward_bases(which, brought):
        scale = jnp.sum(restrict[which][-1] * prolong_weight[0])
        return (returning[which] + brought)[None], scale[None]

    state, terms, carried, echo = close(
        base_sums, every, panel == 0, False, nothing, *forward_bases("A"), "A"
    )
    carried = jnp.where(panel == 0, carried, 0)
    echo = jnp.where(panel == 0, echo, 0)
    brought = {}
    for turn, which in enumerate("ABA"):
        target = turn + 1
        sums_now = cross(terms, turn, target)
        if turn > 0:
            brought[which] = swapped(jnp.stack([carried, echo]), which)
        total = tuple(a + b for a, b in zip(sums_now, base_sums))
        if turn < 2:
            following = "BA"[turn]
            state, terms, new_carried, new_echo = close(
                total, (target,), panel == target, False, state, *forward_bases(following), following
            )
            carried = jnp.where(panel == target, new_carried, carried)
            echo = jnp.where(panel == target, new_echo, echo)
        else:
            entered_echo = by_parity(brought["B"], brought["A"])
            entered = jnp.where(panel > 0, entered_echo[0], 0)
            echoed = entered_echo[1].astype(F32)
            state, terms = close(
                total, (target,), panel == target, False, state, *backward_bases("A", echoed), "A"
            )
    for turn, which in enumerate("ABA"):
        from_panel = PANELS - 1 - turn
        target = from_panel - 1
        sums_now = cross(terms, from_panel, target)
        following = "BAA"[turn]
        state, terms = close(
            sums_now, (target,), panel == target, True, state, *backward_bases(following, echoed), following
        )
        if turn == 1:
            traded_b = swapped(state.astype(BF), "B")
    correction = state

    by_a = swapped(by_parity(last_plane, first_plane), "A")
    by_b = swapped(by_parity(first_plane, last_plane), "B")
    below = jnp.where(panel > 0, by_parity(by_b, by_a), 0)
    above = jnp.where(panel < PANELS - 1, by_parity(by_a, by_b), 0)
    joined_a, joined_b = (jnp.concatenate(traded_leaf[which], axis=1) for which in "AB")
    upper_leaf, lower_leaf = by_parity(joined_a, joined_b), by_parity(joined_b, joined_a)
    enter = times(below, leaf_matrix)
    above_enter = times(last_plane, upper_leaf)
    zhigh = jnp.where(panel < PANELS - 1, above.astype(F32) + above_enter, 0)
    leave = times(zhigh, leaf_matrix)
    below_leave = times(first_plane.astype(F32) + enter, lower_leaf)
    zlow = jnp.where(panel > 0, below.astype(F32) + below_leave, 0)
    left_behind = jnp.where(panel < PANELS - 1, carried, 0)

    below_last = jnp.where(panel > 0, by_parity(prolong["B"], prolong["A"])[-1], 0)
    above_first = jnp.where(panel < PANELS - 1, by_parity(prolong["A"], prolong["B"])[0], 0)

    traded_a = swapped(correction.astype(BF), "A")
    upper = by_parity(traded_a, traded_b)
    lower = by_parity(traded_b, traded_a)
    out_up = times(jnp.concatenate([upper, left_behind], axis=1), leaf_matrix)
    out_down = times(jnp.concatenate([correction.astype(BF), entered], axis=1), lower_leaf)
    out_down = jnp.where(panel > 0, out_down, 0)
    pick = lambda block: (block[:, :sources], block[:, sources:])
    vectors = [correction, entered, upper, lower, left_behind, *pick(out_up), *pick(out_down)]
    vectors = jnp.stack([block.astype(F32) for block in vectors], axis=2)

    scales = jnp.stack([below_last, above_first, prolong_weight[-1]])
    ends = wide(jnp.stack([prolong_weight[:, 0], prolong_weight[:, -1]]))
    near_rows, far_rows = edge_rows(
        flags(True, True), scales, low_rows, high_rows, ends, vectors, enter, leave
    )
    near_front = other_core(near_rows)
    chain = [(p * FRONTS + f, p * FRONTS + (f + 1) % FRONTS) for p in range(PANELS) for f in range(1, FRONTS, 2)]
    far_front = moved(far_rows, pairing(chain))
    xlow = jnp.where(even_core, jnp.where(front > 0, far_front, 0), near_front)
    xhigh = jnp.where(even_core, near_front, jnp.where(front < FRONTS - 1, far_front, 0))
    return tuple(
        finish(
            leaf, source, wave_term, wide(prolong_weight), wide(jnp.stack([below_last, above_first])), vectors,
            enter, leave, xlow, xhigh, zlow, zhigh,
        )
    )


def solution(mesh):
    placed = (
        P(None, None, "panel", "front", None),
        P("panel", "front", None),
        P(None, "panel", "front", None, None),
        P(None, "panel", "front", None, None, None),
        P("panel", "front"),
        P("panel", "front"),
    )
    return jax.shard_map(
        local,
        mesh=mesh,
        in_specs=placed,
        out_specs=(P(None, None, "panel", "front", None), P(None, None, "panel", "front", None)),
        check_vma=False,
    )
```

```python
import functools

import jax
import jax.numpy as jnp
from jax import lax
from jax.experimental import pallas as pl
from jax.experimental.pallas import tpu as pltpu
from jax.sharding import PartitionSpec as P

DAMPING = 0.25
PANELS = 4
FRONTS = 32
AXES = ("panel", "front")
BF = jnp.bfloat16
F32 = jnp.float32
PAIRS = {"A": ((0, 1), (2, 3)), "B": ((1, 2), (0, 3))}


def pairing(swaps):
    target = {}
    for one, two in swaps:
        target[one] = two
        target[two] = one
    for device in range(PANELS * FRONTS):
        target.setdefault(device, device ^ 1)
    return sorted(target.items())


def within(panels, even, odd):
    swaps = []
    for panel in panels:
        for front in range(FRONTS):
            other = front ^ (odd if front % 2 else even)
            swaps.append((panel * FRONTS + front, panel * FRONTS + other))
    return pairing(swaps)


def across(pairs, even, odd):
    swaps = []
    for one, two in pairs:
        for front in range(FRONTS):
            other = front ^ (odd if front % 2 else even)
            swaps.append((one * FRONTS + front, two * FRONTS + other))
    return pairing(swaps)


def moved(block, route):
    return lax.ppermute(block, AXES, route)


def other_core(block):
    return moved(block, pairing(()))


def swapped(block, which):
    return moved(block, across(PAIRS[which], 0, 0))


def product(block, matrix_real, matrix_imag, half):
    by_real = jnp.dot(block, matrix_real, preferred_element_type=F32)
    by_imag = jnp.dot(block, matrix_imag, preferred_element_type=F32)
    return by_real[:half] - by_imag[half:], by_imag[:half] + by_real[half:]


def column(scalars, width):
    row = lax.broadcasted_iota(jnp.int32, (len(scalars), 128), 0)
    tile = jnp.full((len(scalars), 128), scalars[0])
    for i in range(1, len(scalars)):
        tile = jnp.where(row == i, scalars[i], tile)
    return jnp.concatenate([tile] * (width // 128), axis=1)


def dotted(one, two):
    total = one[0] * two[0]
    for a, b in zip(one[1:], two[1:]):
        total = total + a * b
    return total


def entries(ref, kind, plane):
    return [ref[kind, plane, x] for x in range(ref.shape[2])]


def leaf_kernel(weight_ref, source_ref, matrix_ref, leaf_ref, total_ref, first_ref, last_ref, low_ref, high_ref):
    count, planes, rows, width = source_ref.shape[1:]
    flat = count * planes * rows
    real = source_ref[0].reshape(flat, width).astype(BF)
    imag = source_ref[1].reshape(flat, width).astype(BF)
    dot = lambda a, b: jnp.dot(a, b, preferred_element_type=F32)
    out = (
        dot(real, matrix_ref[0]) - dot(imag, matrix_ref[1]),
        dot(real, matrix_ref[1]) + dot(imag, matrix_ref[0]),
    )
    columns = [column(entries(weight_ref, 0, z), width) for z in range(planes)]
    for part in range(2):
        shaped = out[part].reshape(count, planes, rows, width)
        leaf_ref[part] = shaped
        first_ref[part] = shaped[:, 0].astype(BF)
        last_ref[part] = shaped[:, planes - 1].astype(BF)
        low_ref[part] = shaped[:, :, 0]
        high_ref[part] = shaped[:, :, rows - 1]
        total = shaped[:, 0] * columns[0][None]
        for z in range(1, planes):
            total = total + shaped[:, z] * columns[z][None]
        total_ref[0, part] = jnp.sum(total, axis=1)


def leaf_solve(weights, source, matrix):
    two, sources, planes, rows, width = source.shape
    step = 4
    whole = pl.BlockSpec((two, step, planes, rows, width), lambda i: (0, i, 0, 0, 0))
    plane = pl.BlockSpec((two, step, rows, width), lambda i: (0, i, 0, 0))
    leaf, total, first, last, low, high = pl.pallas_call(
        leaf_kernel,
        grid=(sources // step,),
        in_specs=[
            pl.BlockSpec(memory_space=pltpu.SMEM),
            whole,
            pl.BlockSpec((two, width, width), lambda i: (0, 0, 0)),
        ],
        out_specs=[whole, pl.BlockSpec((1, two, step, width), lambda i: (i, 0, 0, 0)), plane, plane, plane, plane],
        out_shape=[
            jax.ShapeDtypeStruct(source.shape, F32),
            jax.ShapeDtypeStruct((sources // step, two, step, width), F32),
            jax.ShapeDtypeStruct((two, sources, rows, width), BF),
            jax.ShapeDtypeStruct((two, sources, rows, width), BF),
            jax.ShapeDtypeStruct((two, sources, planes, width), F32),
            jax.ShapeDtypeStruct((two, sources, planes, width), F32),
        ],
        compiler_params=pltpu.CompilerParams(vmem_limit_bytes=58 * 2**20),
        cost_estimate=pl.CostEstimate(flops=65000000, bytes_accessed=1600000, transcendentals=0),
        name="leaf_solve",
    )(weights, source, matrix)
    return leaf, total.transpose(1, 0, 2, 3).reshape(two, sources, width), first, last, low, high


def whole_call(kernel, shapes, cost, name, smem, *args):
    spaces = [pltpu.SMEM] * smem + [pltpu.VMEM] * (len(args) - smem)
    return pl.pallas_call(
        kernel,
        in_specs=[pl.BlockSpec(memory_space=space) for space in spaces],
        out_specs=[pl.BlockSpec(memory_space=pltpu.VMEM)] * len(shapes),
        out_shape=shapes,
        compiler_params=pltpu.CompilerParams(vmem_limit_bytes=28 * 2**20),
        cost_estimate=pl.CostEstimate(flops=cost, bytes_accessed=cost // 200, transcendentals=0),
        name=name,
    )(*args)


def near_kernel(own_ref, quad_ref, slab_ref, matrix_ref, out_ref):
    sources, width = own_ref.shape[1:]
    total = None
    for level, ref in enumerate((own_ref, quad_ref, slab_ref)):
        block = ref[...].reshape(2 * sources, width).astype(BF)
        got = product(block, matrix_ref[0, level], matrix_ref[1, level], sources)
        total = got if total is None else (total[0] + got[0], total[1] + got[1])
    out_ref[0] = total[0]
    out_ref[1] = total[1]


def near_part(own, quad, slab, separators):
    return whole_call(
        near_kernel, [jax.ShapeDtypeStruct(own.shape, F32)], 150000000, "near_part", 0, own, quad, slab, separators
    )[0]


def advanced(target, keep, place_ref, near_ref, slab_ref, side_ref, opposite_ref, back_ref, before_ref, root_ref, state_ref):
    sources, width = near_ref.shape[1:]
    even = place_ref[0] == 1
    active = place_ref[1] == target
    mine = opposite_ref[...].astype(F32)
    other = back_ref[2].astype(F32)
    root = []
    for part in range(2):
        far = jnp.where(even, mine, other) if part == 0 else jnp.where(even, other, mine)
        root.append(slab_ref[part] + side_ref[part].astype(F32) + back_ref[part].astype(F32) + far)
    block = jnp.concatenate(root, axis=0).astype(BF)
    got = product(block, root_ref[0], root_ref[1], sources)
    state = []
    for part in range(2):
        old = before_ref[part]
        new = near_ref[part] + got[part]
        if keep:
            new = new + old
        state.append(jnp.where(active, new, old))
        state_ref[part] = state[part]
    return state, active


def forward_kernel(
    target, which, place_ref, own_ref, traded_ref, near_ref, slab_ref, side_ref, opposite_ref, back_ref, before_ref,
    root_ref, leaf_ref, sums_ref, parcel_ref, state_ref, terms_ref, out_ref,
):
    state, active = advanced(
        target, False, place_ref, near_ref, slab_ref, side_ref, opposite_ref, back_ref, before_ref, root_ref, state_ref
    )
    sources = near_ref.shape[1]
    end = own_ref.shape[1] - 1
    scale = dotted(entries(traded_ref, 0, 0), entries(own_ref, 1, end))
    own_scale = dotted(entries(own_ref, 0, end), entries(own_ref, 1, end))
    rows = []
    for part in range(2):
        here = state[part]
        rows += [sums_ref["AB".index(which), part] + scale * here, here, sums_ref[2, part] + own_scale * here]
    block = jnp.concatenate(rows, axis=0).astype(BF)
    got = product(block, leaf_ref[0], leaf_ref[1], 3 * sources)
    for part in range(2):
        terms_ref[part] = got[part][:sources].astype(BF)
        for i in range(2):
            new = got[part][(i + 1) * sources : (i + 2) * sources].astype(BF)
            out_ref[i, part] = jnp.where(active, new, parcel_ref[i, part])


def backward_kernel(
    target, keep, which, place_ref, own_ref, traded_ref, near_ref, slab_ref, side_ref, opposite_ref, back_ref, before_ref,
    root_ref, leaf_ref, sums_ref, by_a_ref, by_b_ref, state_ref, terms_ref,
):
    state, _ = advanced(
        target, keep, place_ref, near_ref, slab_ref, side_ref, opposite_ref, back_ref, before_ref, root_ref, state_ref
    )
    sources = near_ref.shape[1]
    end = own_ref.shape[1] - 1
    even_panel = lax.rem(place_ref[1], 2) == 0
    scale = dotted(entries(traded_ref, 0, end), entries(own_ref, 1, 0))
    rows = []
    for part in range(2):
        echo = jnp.where(even_panel, by_b_ref[1, part], by_a_ref[1, part]).astype(F32)
        rows.append(sums_ref[3 + "AB".index(which), part] + echo + scale * state[part])
    block = jnp.concatenate(rows, axis=0).astype(BF)
    got = product(block, leaf_ref[0], leaf_ref[1], sources)
    for part in range(2):
        terms_ref[part] = got[part].astype(BF)


def last_kernel(
    target, place_ref, near_ref, slab_ref, side_ref, opposite_ref, back_ref, before_ref, root_ref, state_ref
):
    advanced(
        target, True, place_ref, near_ref, slab_ref, side_ref, opposite_ref, back_ref, before_ref, root_ref, state_ref
    )


def sums_kernel(own_ref, by_a_ref, by_b_ref, first_ref, last_ref, out_ref):
    width = first_ref.shape[3]
    end = own_ref.shape[1] - 1
    tables = [
        (last_ref, column(entries(by_a_ref, 0, 0), width)),
        (last_ref, column(entries(by_b_ref, 0, 0), width)),
        (last_ref, column(entries(own_ref, 0, end), width)),
        (first_ref, column(entries(by_a_ref, 0, end), width)),
        (first_ref, column(entries(by_b_ref, 0, end), width)),
    ]
    for part in range(2):
        for i, (ref, table) in enumerate(tables):
            out_ref[i, part] = jnp.sum(ref[part].astype(F32) * table[None], axis=1)


def planes_kernel(
    place_ref, by_a_ref, by_b_ref, first_ref, last_ref, own_ref, leaf_a_ref, leaf_b_ref,
    enter_ref, leave_ref, zlow_ref, zhigh_ref,
):
    two, sources, rows, width = first_ref.shape
    flat = sources * rows
    panel = place_ref[1]
    even = lax.rem(panel, 2) == 0
    lower = panel > 0
    upper = panel < PANELS - 1

    def stacked(parts):
        return jnp.concatenate([part.reshape(flat, width) for part in parts], axis=0).astype(BF)

    def times(parts, matrix):
        return [part.reshape(sources, rows, width) for part in product(stacked(parts), matrix[0], matrix[1], flat)]

    below = [jnp.where(even, by_b_ref[part], by_a_ref[part]).astype(F32) for part in range(2)]
    below = [jnp.where(lower, part, 0.0) for part in below]
    above = [jnp.where(even, by_a_ref[part], by_b_ref[part]).astype(F32) for part in range(2)]
    upper_leaf = [jnp.where(even, leaf_a_ref[part], leaf_b_ref[part]) for part in range(2)]
    lower_leaf = [jnp.where(even, leaf_b_ref[part], leaf_a_ref[part]) for part in range(2)]
    own_leaf = [own_ref[0], own_ref[1]]
    enter = times(below, own_leaf)
    above_enter = times([last_ref[part].astype(F32) for part in range(2)], upper_leaf)
    zhigh = [jnp.where(upper, above[part] + above_enter[part], 0.0) for part in range(2)]
    leave = times(zhigh, own_leaf)
    below_leave = times([first_ref[part].astype(F32) + enter[part] for part in range(2)], lower_leaf)
    for part in range(2):
        enter_ref[part] = enter[part]
        leave_ref[part] = leave[part]
        zhigh_ref[part] = zhigh[part]
        zlow_ref[part] = jnp.where(lower, below[part] + below_leave[part], 0.0)


def neighbour_tables(place_ref, by_a_ref, by_b_ref, end):
    panel = place_ref[1]
    even = lax.rem(panel, 2) == 0
    pick = lambda one, two, there: jnp.where(there, jnp.where(even, one, two), 0.0)
    below = [
        pick(b, a, panel > 0) for a, b in zip(entries(by_a_ref, 1, end), entries(by_b_ref, 1, end))
    ]
    above = [
        pick(a, b, panel < PANELS - 1) for a, b in zip(entries(by_a_ref, 1, 0), entries(by_b_ref, 1, 0))
    ]
    return below, above


def closing_kernel(
    place_ref, own_w_ref, a_w_ref, b_w_ref, state_ref, got_a_ref, got_b_ref, parcel_a_ref, parcel_b_ref, parcel_ref,
    own_ref, leaf_a_ref, leaf_b_ref, low_ref, high_ref, enter_ref, leave_ref, vector_ref, near_ref, far_ref,
):
    sources, planes, width = low_ref.shape[1:]
    rows = enter_ref.shape[2]
    panel = place_ref[1]
    even_core = place_ref[0] == 1
    even = lax.rem(panel, 2) == 0
    lower = panel > 0
    upper = panel < PANELS - 1
    below_last, above_first = neighbour_tables(place_ref, a_w_ref, b_w_ref, planes - 1)
    own_last = entries(own_w_ref, 1, planes - 1)
    own_leaf = [own_ref[0], own_ref[1]]
    lower_leaf = [jnp.where(even, leaf_b_ref[part], leaf_a_ref[part]) for part in range(2)]
    here, entered, above, below, behind = [], [], [], [], []
    for part in range(2):
        here.append(state_ref[part])
        entered.append(jnp.where(lower, jnp.where(even, parcel_b_ref[0, part], parcel_a_ref[0, part]).astype(F32), 0.0))
        above.append(jnp.where(even, got_a_ref[part], got_b_ref[part]).astype(F32))
        below.append(jnp.where(even, got_b_ref[part], got_a_ref[part]).astype(F32))
        behind.append(jnp.where(upper, parcel_ref[0, part].astype(F32), 0.0))
    stacked = lambda one, two: jnp.concatenate([one[0], two[0], one[1], two[1]], axis=0).astype(BF)
    out_up = product(stacked(above, behind), own_leaf[0], own_leaf[1], 2 * sources)
    out_down = product(stacked(here, entered), lower_leaf[0], lower_leaf[1], 2 * sources)
    depth = lax.broadcasted_iota(jnp.int32, (planes, width), 0)
    ends = [column([own_w_ref[1, z, x] for z in range(planes)], width) for x in (0, rows - 1)]
    for part in range(2):
        down = jnp.where(lower, out_down[part], 0.0)
        vectors = [
            here[part], entered[part], above[part], below[part], behind[part],
            out_up[part][:sources], out_up[part][sources:], down[:sources], down[sources:],
        ]
        for i, vector in enumerate(vectors):
            vector_ref[part, i] = vector
        for b in range(sources):
            row = lambda i: vector_ref[part, i, b : b + 1]
            done = []
            for side, ref in ((0, low_ref), (1, high_ref)):
                x = 0 if side == 0 else rows - 1
                enter = enter_ref[part, b, x : x + 1] + below_last[x] * row(1)
                leave = leave_ref[part, b, x : x + 1] + above_first[x] * row(5) + own_last[x] * row(6)
                tile = ref[part, b] + ends[side] * row(0)
                tile = tile + jnp.where(depth == 0, enter, 0.0) + jnp.where(depth == planes - 1, leave, 0.0)
                done.append(tile)
            near_ref[part, b] = jnp.where(even_core, done[1], done[0]).astype(BF)
            far_ref[part, b] = jnp.where(even_core, done[0], done[1]).astype(BF)


def final_kernel(
    place_ref, own_w_ref, a_w_ref, b_w_ref, leaf_ref, source_ref, wave_ref, vector_ref, enter_ref, leave_ref,
    near_ref, far_ref, zlow_ref, zhigh_ref, field_ref, residual_ref,
):
    count, planes, rows, width = leaf_ref.shape[1:]
    lane = lax.broadcasted_iota(jnp.int32, (rows, width), 1)
    row = lax.broadcasted_iota(jnp.int32, (rows, width), 0)
    even_core = place_ref[0] == 1
    low_there = place_ref[2] > 0
    high_there = place_ref[2] < FRONTS - 1
    below_last, above_first = (
        column(table, width) for table in neighbour_tables(place_ref, a_w_ref, b_w_ref, planes - 1)
    )
    prolong = [column(entries(own_w_ref, 1, z), width) for z in range(planes)]
    own_last, own_first = prolong[planes - 1], prolong[0]
    start = pl.program_id(0) * count
    for b in range(count):
        field, ends = [], []
        for part in range(2):
            vec = [vector_ref[part, i, pl.ds(start + b, 1)] for i in range(9)]
            tiles = []
            for z in range(planes):
                tile = leaf_ref[part, b, z] + prolong[z] * vec[0]
                if z == 0:
                    tile = tile + enter_ref[part, b] + below_last * vec[1]
                if z == planes - 1:
                    tile = tile + leave_ref[part, b] + above_first * vec[5] + own_last * vec[6]
                field_ref[part, b, z] = tile
                tiles.append(tile)
            field.append(tiles)
            below = zlow_ref[part, b] + below_last * (vec[3] + vec[8]) + own_first * vec[7]
            above = zhigh_ref[part, b] + above_first * vec[2] + own_last * vec[4]
            ends.append((below, above))
        for part in range(2):
            tiles = field[part]
            near_rows = near_ref[part, b].astype(F32)
            far_rows = far_ref[part, b].astype(F32)
            low_rows = jnp.where(even_core, jnp.where(low_there, far_rows, 0.0), near_rows)
            high_rows = jnp.where(even_core, near_rows, jnp.where(high_there, far_rows, 0.0))
            for z in range(planes):
                diag_real = 6.0 - wave_ref[z]
                diag_imag = -DAMPING * wave_ref[z]
                here = tiles[z]
                below = tiles[z - 1] if z else ends[part][0]
                above = tiles[z + 1] if z < planes - 1 else ends[part][1]
                near = below + above
                low = jnp.where(row == 0, low_rows[z : z + 1], pltpu.roll(here, 1, 0))
                high = jnp.where(row == rows - 1, high_rows[z : z + 1], pltpu.roll(here, rows - 1, 0))
                near = near + low + high
                left = jnp.where(lane == 0, 0.0, pltpu.roll(here, 1, 1))
                right = jnp.where(lane == width - 1, 0.0, pltpu.roll(here, width - 1, 1))
                near = near + left + right
                cross = diag_imag * field[1 - part][z]
                applied = diag_real * here - near
                applied = applied - cross if part == 0 else applied + cross
                residual_ref[part, b, z] = source_ref[part, b, z] - applied


def finish(scalars, leaf, source, wave_term, vectors, *planes_in):
    two, sources, planes, rows, width = source.shape
    step = 2
    whole = pl.BlockSpec((two, step, planes, rows, width), lambda i: (0, i, 0, 0, 0))
    plane = pl.BlockSpec((two, step, rows, width), lambda i: (0, i, 0, 0))
    return pl.pallas_call(
        final_kernel,
        grid=(sources // step,),
        in_specs=[pl.BlockSpec(memory_space=pltpu.SMEM)] * 4
        + [
            whole, whole,
            pl.BlockSpec((planes, rows, width), lambda i: (0, 0, 0)),
            pl.BlockSpec(vectors.shape, lambda i: (0, 0, 0, 0)),
            plane, plane, plane, plane, plane, plane,
        ],
        out_specs=[whole, whole],
        out_shape=[jax.ShapeDtypeStruct(source.shape, F32)] * 2,
        compiler_params=pltpu.CompilerParams(vmem_limit_bytes=58 * 2**20),
        cost_estimate=pl.CostEstimate(flops=60000000, bytes_accessed=26000000, transcendentals=0),
        name="finish",
    )(*scalars, leaf, source, wave_term, vectors, *planes_in)


def after(value, *others):
    return lax.optimization_barrier((value, *others))[0]


def local(source, wave_term, leaf_inverse, separator_inverse, restrict_weight, prolong_weight):
    two, sources, planes, rows, width = source.shape
    panel = lax.axis_index("panel")
    front = lax.axis_index("front")
    even_core = front % 2 == 0
    even_panel = panel % 2 == 0
    leaf_matrix = leaf_inverse[:, 0, 0]
    separators = separator_inverse[:, 0, 0]
    root_matrix = separators[:, 3]
    place = jnp.stack([even_core.astype(jnp.int32), panel, front])
    vector = (two, sources, width)
    shape = jax.ShapeDtypeStruct

    weights = jnp.stack([restrict_weight, prolong_weight])
    traded_leaf = {which: swapped(leaf_matrix, which) for which in "AB"}
    traded_weights = {which: swapped(weights, which) for which in "AB"}
    leaf, base_terms, first_plane, last_plane, low_rows, high_rows = leaf_solve(weights, source, leaf_matrix)

    def halves(block):
        return jnp.where(even_core, block[0], block[1])

    def inside(sent, panels, near, far, cross):
        side = moved(sent, within(panels, near, cross))
        opposite = moved(halves(sent), within(panels, far, far))
        back = other_core(jnp.concatenate([side, opposite[None]]))
        return side, opposite, back

    def pair_sum(terms):
        return terms.astype(F32) + other_core(terms).astype(F32)

    every = tuple(range(PANELS))
    pair = pair_sum(base_terms.astype(BF))
    side, opposite, back = inside(pair.astype(BF), every, 2, 4, 6)
    near_term = jnp.where(even_core, side, back[:2]).astype(F32)
    far_term = jnp.where(even_core, jnp.stack([opposite, back[2]]), jnp.stack([back[2], opposite])).astype(F32)
    quad = pair + near_term
    slab = pair + side.astype(F32) + back[:2].astype(F32) + far_term
    slab = after(slab, traded_leaf["A"], traded_leaf["B"])
    base_sums = (pair, quad, slab)
    nothing = jnp.zeros(vector, F32)

    sums = whole_call(
        sums_kernel, [shape((5,) + vector, F32)], 10000000, "edge_sums", 3,
        weights, traded_weights["A"], traded_weights["B"], first_plane, last_plane,
    )[0]

    def gather(level_sums, panels, before):
        own, quad, slab = level_sums
        near = near_part(own, quad, slab, separators)
        return (near, slab, *inside(slab.astype(BF), panels, 8, 16, 24), before, root_matrix)

    def forward_close(level_sums, panels, target, which, before, parcel):
        got = gather(level_sums, panels, before)
        return whole_call(
            functools.partial(forward_kernel, target, which),
            [shape(vector, F32), shape(vector, BF), shape((2,) + vector, BF)], 200000000, "forward", 3,
            place, weights, traded_weights[which], *got, traded_leaf[which], sums, parcel,
        )

    def backward_close(level_sums, panels, target, keep, which, before, brought):
        got = gather(level_sums, panels, before)
        return whole_call(
            functools.partial(backward_kernel, target, keep, which),
            [shape(vector, F32), shape(vector, BF)], 200000000, "backward", 3,
            place, weights, traded_weights[which], *got, traded_leaf[which], sums, brought["A"], brought["B"],
        )

    def cross(terms, from_panel, to_panel):
        sent = pair_sum(terms).astype(BF)
        ends = ((from_panel, to_panel),)
        one = moved(sent, across(ends, 0, 2))
        two_ = moved(sent, across(ends, 4, 6))
        back = other_core(jnp.stack([one, two_])).astype(F32)
        one = one.astype(F32)
        own = jnp.where(even_core, one, back[0])
        quad = one + back[0]
        return own, quad, quad + two_.astype(F32) + back[1]

    state, terms, parcel = forward_close(base_sums, every, 0, "A", nothing, jnp.zeros((2,) + vector, BF))
    brought = {}
    for turn, which in enumerate("ABA"):
        target = turn + 1
        sums_now = cross(terms, turn, target)
        if turn > 0:
            brought[which] = swapped(parcel, which)
        total = tuple(a + b for a, b in zip(sums_now, base_sums))
        if turn < 2:
            state, terms, parcel = forward_close(total, (target,), target, "BA"[turn], state, parcel)
        else:
            state, terms = backward_close(total, (target,), target, False, "A", state, brought)
    for turn in range(PANELS - 1):
        from_panel = PANELS - 1 - turn
        target = from_panel - 1
        sums_now = cross(terms, from_panel, target)
        if turn < PANELS - 2:
            state, terms = backward_close(sums_now, (target,), target, True, "BA"[turn], state, brought)
        else:
            got = gather(sums_now, (target,), state)
            state = whole_call(
                functools.partial(last_kernel, target), [shape(vector, F32)], 100000000, "last", 1, place, *got
            )[0]
        if turn == 1:
            traded_b = swapped(state.astype(BF), "B")
    traded_a = swapped(state.astype(BF), "A")

    def by_parity(even_value, odd_value):
        return jnp.where(even_panel, even_value, odd_value)

    by_a = swapped(by_parity(last_plane, first_plane), "A")
    by_b = swapped(by_parity(first_plane, last_plane), "B")
    plane = shape(first_plane.shape, F32)
    enter, leave, zlow, zhigh = whole_call(
        planes_kernel, [plane] * 4, 400000000, "planes", 1,
        place, by_a, by_b, first_plane, last_plane, leaf_matrix, traded_leaf["A"], traded_leaf["B"],
    )
    scalars = (place, weights, traded_weights["A"], traded_weights["B"])
    edge = shape(low_rows.shape, BF)
    vectors, near_rows, far_rows = whole_call(
        closing_kernel, [shape((two, 9, sources, width), F32), edge, edge], 300000000, "closing", 4,
        *scalars, state, traded_a, traded_b, brought["A"], brought["B"], parcel,
        leaf_matrix, traded_leaf["A"], traded_leaf["B"], low_rows, high_rows, enter, leave,
    )
    near_front = other_core(near_rows)
    chain = [(p * FRONTS + f, p * FRONTS + (f + 1) % FRONTS) for p in range(PANELS) for f in range(1, FRONTS, 2)]
    far_front = moved(far_rows, pairing(chain))
    return tuple(
        finish(scalars, leaf, source, wave_term, vectors, enter, leave, near_front, far_front, zlow, zhigh)
    )


def solution(mesh):
    placed = (
        P(None, None, "panel", "front", None),
        P("panel", "front", None),
        P(None, "panel", "front", None, None),
        P(None, "panel", "front", None, None, None),
        P("panel", "front"),
        P("panel", "front"),
    )
    return jax.shard_map(
        local,
        mesh=mesh,
        in_specs=placed,
        out_specs=(P(None, None, "panel", "front", None), P(None, None, "panel", "front", None)),
        check_vma=False,
    )
```

```python
import functools

import jax
import jax.numpy as jnp
from jax import lax
from jax.experimental import pallas as pl
from jax.experimental.pallas import tpu as pltpu
from jax.sharding import PartitionSpec as P

DAMPING = 0.25
PANELS = 4
FRONTS = 32
AXES = ("panel", "front")
BF = jnp.bfloat16
F32 = jnp.float32
PAIRS = {"A": ((0, 1), (2, 3)), "B": ((1, 2), (0, 3))}


def pairing(swaps):
    target = {}
    for one, two in swaps:
        target[one] = two
        target[two] = one
    for device in range(PANELS * FRONTS):
        target.setdefault(device, device ^ 1)
    return sorted(target.items())


def within(panels, even, odd):
    swaps = []
    for panel in panels:
        for front in range(FRONTS):
            other = front ^ (odd if front % 2 else even)
            swaps.append((panel * FRONTS + front, panel * FRONTS + other))
    return pairing(swaps)


def across(pairs, even, odd):
    swaps = []
    for one, two in pairs:
        for front in range(FRONTS):
            other = front ^ (odd if front % 2 else even)
            swaps.append((one * FRONTS + front, two * FRONTS + other))
    return pairing(swaps)


def moved(block, route):
    return lax.ppermute(block, AXES, route)


def other_core(block):
    return moved(block, pairing(()))


def swapped(block, which):
    return moved(block, across(PAIRS[which], 0, 0))


def product(block, matrix_real, matrix_imag, half):
    by_real = jnp.dot(block, matrix_real, preferred_element_type=F32)
    by_imag = jnp.dot(block, matrix_imag, preferred_element_type=F32)
    return by_real[:half] - by_imag[half:], by_imag[:half] + by_real[half:]


def column(scalars, width):
    row = lax.broadcasted_iota(jnp.int32, (len(scalars), 128), 0)
    tile = jnp.full((len(scalars), 128), scalars[0])
    for i in range(1, len(scalars)):
        tile = jnp.where(row == i, scalars[i], tile)
    return jnp.concatenate([tile] * (width // 128), axis=1)


def dotted(one, two):
    total = one[0] * two[0]
    for a, b in zip(one[1:], two[1:]):
        total = total + a * b
    return total


def entries(ref, kind, plane):
    return [ref[kind, plane, x] for x in range(ref.shape[2])]


def leaf_kernel(weight_ref, source_ref, matrix_ref, leaf_ref, total_ref, first_ref, last_ref, low_ref, high_ref):
    count, planes, rows, width = source_ref.shape[1:]
    flat = count * planes * rows
    real = source_ref[0].reshape(flat, width).astype(BF)
    imag = source_ref[1].reshape(flat, width).astype(BF)
    dot = lambda a, b: jnp.dot(a, b, preferred_element_type=F32)
    out = (
        dot(real, matrix_ref[0]) - dot(imag, matrix_ref[1]),
        dot(real, matrix_ref[1]) + dot(imag, matrix_ref[0]),
    )
    columns = [column(entries(weight_ref, 0, z), width) for z in range(planes)]
    for part in range(2):
        shaped = out[part].reshape(count, planes, rows, width)
        leaf_ref[part] = shaped
        first_ref[part] = shaped[:, 0].astype(BF)
        last_ref[part] = shaped[:, planes - 1].astype(BF)
        low_ref[part] = shaped[:, :, 0]
        high_ref[part] = shaped[:, :, rows - 1]
        total = shaped[:, 0] * columns[0][None]
        for z in range(1, planes):
            total = total + shaped[:, z] * columns[z][None]
        total_ref[0, part] = jnp.sum(total, axis=1)


def leaf_solve(weights, source, matrix):
    two, sources, planes, rows, width = source.shape
    step = 6
    whole = pl.BlockSpec((two, step, planes, rows, width), lambda i: (0, i, 0, 0, 0))
    plane = pl.BlockSpec((two, step, rows, width), lambda i: (0, i, 0, 0))
    leaf, total, first, last, low, high = pl.pallas_call(
        leaf_kernel,
        grid=(sources // step,),
        in_specs=[
            pl.BlockSpec(memory_space=pltpu.SMEM),
            whole,
            pl.BlockSpec((two, width, width), lambda i: (0, 0, 0)),
        ],
        out_specs=[whole, pl.BlockSpec((1, two, step, width), lambda i: (i, 0, 0, 0)), plane, plane, plane, plane],
        out_shape=[
            pltpu.HBM(source.shape, F32),
            jax.ShapeDtypeStruct((sources // step, two, step, width), F32),
            jax.ShapeDtypeStruct((two, sources, rows, width), BF),
            jax.ShapeDtypeStruct((two, sources, rows, width), BF),
            jax.ShapeDtypeStruct((two, sources, planes, width), F32),
            jax.ShapeDtypeStruct((two, sources, planes, width), F32),
        ],
        compiler_params=pltpu.CompilerParams(vmem_limit_bytes=32 * 2**20),
        cost_estimate=pl.CostEstimate(flops=65000000, bytes_accessed=1600000, transcendentals=0),
        name="leaf_solve",
    )(weights, source, matrix)
    return leaf, total.transpose(1, 0, 2, 3).reshape(two, sources, width), first, last, low, high


def whole_call(kernel, shapes, cost, name, smem, *args, limit=14):
    spaces = [pltpu.SMEM] * smem + [pltpu.VMEM] * (len(args) - smem)
    return pl.pallas_call(
        kernel,
        in_specs=[pl.BlockSpec(memory_space=space) for space in spaces],
        out_specs=[pl.BlockSpec(memory_space=pltpu.VMEM)] * len(shapes),
        out_shape=shapes,
        compiler_params=pltpu.CompilerParams(vmem_limit_bytes=limit * 2**20),
        cost_estimate=pl.CostEstimate(flops=cost, bytes_accessed=cost // 200, transcendentals=0),
        name=name,
    )(*args)


def near_kernel(own_ref, quad_ref, slab_ref, matrix_ref, out_ref):
    sources, width = own_ref.shape[1:]
    total = None
    for level, ref in enumerate((own_ref, quad_ref, slab_ref)):
        block = ref[...].reshape(2 * sources, width).astype(BF)
        got = product(block, matrix_ref[0, level], matrix_ref[1, level], sources)
        total = got if total is None else (total[0] + got[0], total[1] + got[1])
    out_ref[0] = total[0]
    out_ref[1] = total[1]


def near_part(own, quad, slab, separators):
    return whole_call(
        near_kernel, [jax.ShapeDtypeStruct(own.shape, F32)], 150000000, "near_part", 0, own, quad, slab, separators
    )[0]


def advanced(target, keep, place_ref, near_ref, slab_ref, side_ref, opposite_ref, back_ref, before_ref, root_ref, state_ref):
    sources, width = near_ref.shape[1:]
    even = place_ref[0] == 1
    active = place_ref[1] == target
    mine = opposite_ref[...].astype(F32)
    other = back_ref[2].astype(F32)
    root = []
    for part in range(2):
        far = jnp.where(even, mine, other) if part == 0 else jnp.where(even, other, mine)
        root.append(slab_ref[part] + side_ref[part].astype(F32) + back_ref[part].astype(F32) + far)
    block = jnp.concatenate(root, axis=0).astype(BF)
    got = product(block, root_ref[0, 3], root_ref[1, 3], sources)
    state = []
    for part in range(2):
        old = before_ref[part]
        new = near_ref[part] + got[part]
        if keep:
            new = new + old
        state.append(jnp.where(active, new, old))
        state_ref[part] = state[part]
    return state, active


def forward_kernel(
    target, which, place_ref, own_ref, traded_ref, near_ref, slab_ref, side_ref, opposite_ref, back_ref, before_ref,
    root_ref, leaf_ref, sums_ref, parcel_ref, state_ref, terms_ref, out_ref,
):
    state, active = advanced(
        target, False, place_ref, near_ref, slab_ref, side_ref, opposite_ref, back_ref, before_ref, root_ref, state_ref
    )
    sources = near_ref.shape[1]
    end = own_ref.shape[1] - 1
    scale = dotted(entries(traded_ref, 0, 0), entries(own_ref, 1, end))
    own_scale = dotted(entries(own_ref, 0, end), entries(own_ref, 1, end))
    rows = []
    for part in range(2):
        here = state[part]
        rows += [sums_ref["AB".index(which), part] + scale * here, here, sums_ref[2, part] + own_scale * here]
    block = jnp.concatenate(rows, axis=0).astype(BF)
    got = product(block, leaf_ref[0], leaf_ref[1], 3 * sources)
    for part in range(2):
        terms_ref[part] = got[part][:sources].astype(BF)
        for i in range(2):
            new = got[part][(i + 1) * sources : (i + 2) * sources].astype(BF)
            out_ref[i, part] = jnp.where(active, new, parcel_ref[i, part])


def backward_kernel(
    target, keep, which, place_ref, own_ref, traded_ref, near_ref, slab_ref, side_ref, opposite_ref, back_ref, before_ref,
    root_ref, leaf_ref, sums_ref, by_a_ref, by_b_ref, state_ref, terms_ref,
):
    state, _ = advanced(
        target, keep, place_ref, near_ref, slab_ref, side_ref, opposite_ref, back_ref, before_ref, root_ref, state_ref
    )
    sources = near_ref.shape[1]
    end = own_ref.shape[1] - 1
    even_panel = lax.rem(place_ref[1], 2) == 0
    scale = dotted(entries(traded_ref, 0, end), entries(own_ref, 1, 0))
    rows = []
    for part in range(2):
        echo = jnp.where(even_panel, by_b_ref[1, part], by_a_ref[1, part]).astype(F32)
        rows.append(sums_ref[3 + "AB".index(which), part] + echo + scale * state[part])
    block = jnp.concatenate(rows, axis=0).astype(BF)
    got = product(block, leaf_ref[0], leaf_ref[1], sources)
    for part in range(2):
        terms_ref[part] = got[part].astype(BF)


def sums_kernel(own_ref, by_a_ref, by_b_ref, first_ref, last_ref, out_ref):
    width = first_ref.shape[3]
    end = own_ref.shape[1] - 1
    tables = [
        (last_ref, column(entries(by_a_ref, 0, 0), width)),
        (last_ref, column(entries(by_b_ref, 0, 0), width)),
        (last_ref, column(entries(own_ref, 0, end), width)),
        (first_ref, column(entries(by_a_ref, 0, end), width)),
        (first_ref, column(entries(by_b_ref, 0, end), width)),
    ]
    for part in range(2):
        for i, (ref, table) in enumerate(tables):
            out_ref[i, part] = jnp.sum(ref[part].astype(F32) * table[None], axis=1)


def planes_kernel(
    place_ref, by_a_ref, by_b_ref, first_ref, last_ref, own_ref, leaf_a_ref, leaf_b_ref,
    enter_ref, leave_ref, zlow_ref, zhigh_ref,
):
    two, sources, rows, width = first_ref.shape
    flat = sources * rows
    panel = place_ref[1]
    even = lax.rem(panel, 2) == 0
    lower = panel > 0
    upper = panel < PANELS - 1

    def stacked(parts):
        return jnp.concatenate([part.reshape(flat, width) for part in parts], axis=0).astype(BF)

    def times(parts, matrix):
        return [part.reshape(sources, rows, width) for part in product(stacked(parts), matrix[0], matrix[1], flat)]

    below = [jnp.where(even, by_b_ref[part], by_a_ref[part]).astype(F32) for part in range(2)]
    below = [jnp.where(lower, part, 0.0) for part in below]
    above = [jnp.where(even, by_a_ref[part], by_b_ref[part]).astype(F32) for part in range(2)]
    upper_leaf = [jnp.where(even, leaf_a_ref[part], leaf_b_ref[part]) for part in range(2)]
    lower_leaf = [jnp.where(even, leaf_b_ref[part], leaf_a_ref[part]) for part in range(2)]
    own_leaf = [own_ref[0], own_ref[1]]
    enter = times(below, own_leaf)
    above_enter = times([last_ref[part].astype(F32) for part in range(2)], upper_leaf)
    zhigh = [jnp.where(upper, above[part] + above_enter[part], 0.0) for part in range(2)]
    leave = times(zhigh, own_leaf)
    below_leave = times([first_ref[part].astype(F32) + enter[part] for part in range(2)], lower_leaf)
    for part in range(2):
        enter_ref[part] = enter[part]
        leave_ref[part] = leave[part]
        zhigh_ref[part] = zhigh[part]
        zlow_ref[part] = jnp.where(lower, below[part] + below_leave[part], 0.0)


def neighbour_tables(place_ref, by_a_ref, by_b_ref, end):
    panel = place_ref[1]
    even = lax.rem(panel, 2) == 0
    pick = lambda one, two, there: jnp.where(there, jnp.where(even, one, two), 0.0)
    below = [
        pick(b, a, panel > 0) for a, b in zip(entries(by_a_ref, 1, end), entries(by_b_ref, 1, end))
    ]
    above = [
        pick(a, b, panel < PANELS - 1) for a, b in zip(entries(by_a_ref, 1, 0), entries(by_b_ref, 1, 0))
    ]
    return below, above


def closing_kernel(
    target, place_ref, own_w_ref, a_w_ref, b_w_ref, near_ref, slab_ref, side_ref, opposite_ref, back_ref, before_ref,
    root_ref, got_a_ref, got_b_ref, parcel_a_ref, parcel_b_ref, parcel_ref, own_ref, leaf_a_ref, leaf_b_ref,
    low_ref, high_ref, enter_ref, leave_ref, state_ref, vector_ref, near_rows_ref, far_rows_ref,
):
    here, _ = advanced(
        target, True, place_ref, near_ref, slab_ref, side_ref, opposite_ref, back_ref, before_ref, root_ref, state_ref
    )
    sources, planes, width = low_ref.shape[1:]
    rows = enter_ref.shape[2]
    panel = place_ref[1]
    even_core = place_ref[0] == 1
    even = lax.rem(panel, 2) == 0
    lower = panel > 0
    upper = panel < PANELS - 1
    below_last, above_first = neighbour_tables(place_ref, a_w_ref, b_w_ref, planes - 1)
    own_last = entries(own_w_ref, 1, planes - 1)
    own_leaf = [own_ref[0], own_ref[1]]
    lower_leaf = [jnp.where(even, leaf_b_ref[part], leaf_a_ref[part]) for part in range(2)]
    entered, above, below, behind = [], [], [], []
    for part in range(2):
        entered.append(jnp.where(lower, jnp.where(even, parcel_b_ref[0, part], parcel_a_ref[0, part]).astype(F32), 0.0))
        above.append(jnp.where(even, got_a_ref[part], got_b_ref[part]).astype(F32))
        below.append(jnp.where(even, got_b_ref[part], got_a_ref[part]).astype(F32))
        behind.append(jnp.where(upper, parcel_ref[0, part].astype(F32), 0.0))
    stacked = lambda one, two: jnp.concatenate([one[0], two[0], one[1], two[1]], axis=0).astype(BF)
    out_up = product(stacked(above, behind), own_leaf[0], own_leaf[1], 2 * sources)
    out_down = product(stacked(here, entered), lower_leaf[0], lower_leaf[1], 2 * sources)
    depth = lax.broadcasted_iota(jnp.int32, (planes, width), 0)
    ends = [column([own_w_ref[1, z, x] for z in range(planes)], width) for x in (0, rows - 1)]
    for part in range(2):
        down = jnp.where(lower, out_down[part], 0.0)
        vectors = [
            here[part], entered[part], above[part], below[part], behind[part],
            out_up[part][:sources], out_up[part][sources:], down[:sources], down[sources:],
        ]
        for i, vector in enumerate(vectors):
            vector_ref[part, i] = vector
        for b in range(sources):
            row = lambda i: vector_ref[part, i, b : b + 1]
            done = []
            for side, ref in ((0, low_ref), (1, high_ref)):
                x = 0 if side == 0 else rows - 1
                enter = enter_ref[part, b, x : x + 1] + below_last[x] * row(1)
                leave = leave_ref[part, b, x : x + 1] + above_first[x] * row(5) + own_last[x] * row(6)
                tile = ref[part, b] + ends[side] * row(0)
                tile = tile + jnp.where(depth == 0, enter, 0.0) + jnp.where(depth == planes - 1, leave, 0.0)
                done.append(tile)
            near_rows_ref[part, b] = jnp.where(even_core, done[1], done[0]).astype(BF)
            far_rows_ref[part, b] = jnp.where(even_core, done[0], done[1]).astype(BF)


def final_kernel(
    place_ref, own_w_ref, a_w_ref, b_w_ref, leaf_ref, source_ref, wave_ref, vector_ref, late_ref, enter_ref, leave_ref,
    near_ref, far_ref, zlow_ref, zhigh_ref, field_ref, residual_ref,
):
    count, planes, rows, width = leaf_ref.shape[1:]
    lane = lax.broadcasted_iota(jnp.int32, (rows, width), 1)
    row = lax.broadcasted_iota(jnp.int32, (rows, width), 0)
    even_core = place_ref[0] == 1
    low_there = place_ref[2] > 0
    high_there = place_ref[2] < FRONTS - 1
    below_last, above_first = (
        column(table, width) for table in neighbour_tables(place_ref, a_w_ref, b_w_ref, planes - 1)
    )
    prolong = [column(entries(own_w_ref, 1, z), width) for z in range(planes)]
    own_last, own_first = prolong[planes - 1], prolong[0]
    even = lax.rem(place_ref[1], 2) == 0
    start = pl.program_id(0) * count
    for b in range(count):
        at = start + b
        field, ends = [], []
        for part in range(2):
            vec = [vector_ref[part, i, pl.ds(at, 1)] for i in range(9)]
            lower = jnp.where(even, vec[3], late_ref[part, pl.ds(at, 1)])
            tiles = []
            for z in range(planes):
                tile = leaf_ref[part, b, z] + prolong[z] * vec[0]
                if z == 0:
                    tile = tile + enter_ref[part, at] + below_last * vec[1]
                if z == planes - 1:
                    tile = tile + leave_ref[part, at] + above_first * vec[5] + own_last * vec[6]
                field_ref[part, b, z] = tile
                tiles.append(tile)
            field.append(tiles)
            below = zlow_ref[part, at] + below_last * (lower + vec[8]) + own_first * vec[7]
            above = zhigh_ref[part, at] + above_first * vec[2] + own_last * vec[4]
            ends.append((below, above))
        for part in range(2):
            tiles = field[part]
            near_rows = near_ref[part, at].astype(F32)
            far_rows = far_ref[part, at].astype(F32)
            low_rows = jnp.where(even_core, jnp.where(low_there, far_rows, 0.0), near_rows)
            high_rows = jnp.where(even_core, near_rows, jnp.where(high_there, far_rows, 0.0))
            for z in range(planes):
                diag_real = 6.0 - wave_ref[z]
                diag_imag = -DAMPING * wave_ref[z]
                here = tiles[z]
                below = tiles[z - 1] if z else ends[part][0]
                above = tiles[z + 1] if z < planes - 1 else ends[part][1]
                near = below + above
                low = jnp.where(row == 0, low_rows[z : z + 1], pltpu.roll(here, 1, 0))
                high = jnp.where(row == rows - 1, high_rows[z : z + 1], pltpu.roll(here, rows - 1, 0))
                near = near + low + high
                left = jnp.where(lane == 0, 0.0, pltpu.roll(here, 1, 1))
                right = jnp.where(lane == width - 1, 0.0, pltpu.roll(here, width - 1, 1))
                near = near + left + right
                cross = diag_imag * field[1 - part][z]
                applied = diag_real * here - near
                applied = applied - cross if part == 0 else applied + cross
                residual_ref[part, b, z] = source_ref[part, b, z] - applied


def finish(scalars, leaf, source, *others):
    two, sources, planes, rows, width = source.shape
    step = 4
    whole = pl.BlockSpec((two, step, planes, rows, width), lambda i: (0, i, 0, 0, 0))
    return pl.pallas_call(
        final_kernel,
        grid=(sources // step,),
        in_specs=[pl.BlockSpec(memory_space=pltpu.SMEM)] * len(scalars)
        + [whole, whole]
        + [pl.BlockSpec(memory_space=pltpu.VMEM)] * len(others),
        out_specs=[whole, whole],
        out_shape=[jax.ShapeDtypeStruct(source.shape, F32)] * 2,
        compiler_params=pltpu.CompilerParams(vmem_limit_bytes=40 * 2**20),
        cost_estimate=pl.CostEstimate(flops=60000000, bytes_accessed=26000000, transcendentals=0),
        name="finish",
    )(*scalars, leaf, source, *others)


def after(value, *others):
    return lax.optimization_barrier((value, *others))[0]


def local(source, wave_term, leaf_inverse, separator_inverse, restrict_weight, prolong_weight):
    two, sources, planes, rows, width = source.shape
    panel = lax.axis_index("panel")
    front = lax.axis_index("front")
    even_core = front % 2 == 0
    even_panel = panel % 2 == 0
    leaf_matrix = leaf_inverse[:, 0, 0]
    separators = separator_inverse[:, 0, 0]
    place = jnp.stack([even_core.astype(jnp.int32), panel, front])
    vector = (two, sources, width)
    shape = jax.ShapeDtypeStruct

    weights = jnp.stack([restrict_weight, prolong_weight])
    traded_leaf = {which: swapped(leaf_matrix, which) for which in "AB"}
    traded_weights = {which: swapped(weights, which) for which in "AB"}
    leaf, base_terms, first_plane, last_plane, low_rows, high_rows = leaf_solve(weights, source, leaf_matrix)
    base_terms = after(base_terms, traded_weights["A"], traded_weights["B"])

    def by_parity(even_value, odd_value):
        return jnp.where(even_panel, even_value, odd_value)

    by_a = swapped(by_parity(last_plane, first_plane), "A")
    by_b = swapped(by_parity(first_plane, last_plane), "B")
    plane = shape(first_plane.shape, F32)
    planes_got = whole_call(
        planes_kernel, [plane] * 4, 400000000, "planes", 1,
        place, by_a, by_b, first_plane, last_plane, leaf_matrix, traded_leaf["A"], traded_leaf["B"], limit=32,
    )

    def halves(block):
        return jnp.where(even_core, block[0], block[1])

    def inside(sent, panels, near, far, cross):
        side = moved(sent, within(panels, near, cross))
        opposite = moved(halves(sent), within(panels, far, far))
        back = other_core(jnp.concatenate([side, opposite[None]]))
        return side, opposite, back

    def pair_sum(terms):
        return terms.astype(F32) + other_core(terms).astype(F32)

    every = tuple(range(PANELS))
    pair = pair_sum(base_terms.astype(BF))
    side, opposite, back = inside(pair.astype(BF), every, 2, 4, 6)
    near_term = jnp.where(even_core, side, back[:2]).astype(F32)
    far_term = jnp.where(even_core, jnp.stack([opposite, back[2]]), jnp.stack([back[2], opposite])).astype(F32)
    quad = pair + near_term
    slab = pair + side.astype(F32) + back[:2].astype(F32) + far_term
    slab = after(slab, traded_leaf["A"], traded_leaf["B"])
    base_sums = (pair, quad, slab)
    nothing = jnp.zeros(vector, F32)

    sums = whole_call(
        sums_kernel, [shape((5,) + vector, F32)], 10000000, "edge_sums", 3,
        weights, traded_weights["A"], traded_weights["B"], first_plane, last_plane,
    )[0]

    def gather(level_sums, panels, before):
        own, quad, slab = level_sums
        near = near_part(own, quad, slab, separators)
        return (near, slab, *inside(slab.astype(BF), panels, 8, 16, 24), before, separators)

    def forward_close(level_sums, panels, target, which, before, parcel):
        got = gather(level_sums, panels, before)
        return whole_call(
            functools.partial(forward_kernel, target, which),
            [shape(vector, F32), shape(vector, BF), shape((2,) + vector, BF)], 200000000, "forward", 3,
            place, weights, traded_weights[which], *got, traded_leaf[which], sums, parcel,
        )

    def backward_close(level_sums, panels, target, keep, which, before, brought):
        got = gather(level_sums, panels, before)
        return whole_call(
            functools.partial(backward_kernel, target, keep, which),
            [shape(vector, F32), shape(vector, BF)], 200000000, "backward", 3,
            place, weights, traded_weights[which], *got, traded_leaf[which], sums, brought["A"], brought["B"],
        )

    def cross(terms, from_panel, to_panel):
        sent = pair_sum(terms).astype(BF)
        ends = ((from_panel, to_panel),)
        one = moved(sent, across(ends, 0, 2))
        two_ = moved(sent, across(ends, 4, 6))
        back = other_core(jnp.stack([one, two_])).astype(F32)
        one = one.astype(F32)
        own = jnp.where(even_core, one, back[0])
        quad = one + back[0]
        return own, quad, quad + two_.astype(F32) + back[1]

    state, terms, parcel = forward_close(base_sums, every, 0, "A", nothing, jnp.zeros((2,) + vector, BF))
    brought = {}
    for turn, which in enumerate("ABA"):
        target = turn + 1
        sums_now = cross(terms, turn, target)
        if turn > 0:
            brought[which] = swapped(parcel, which)
        total = tuple(a + b for a, b in zip(sums_now, base_sums))
        if turn < 2:
            state, terms, parcel = forward_close(total, (target,), target, "BA"[turn], state, parcel)
        else:
            state, terms = backward_close(total, (target,), target, False, "A", state, brought)
        if turn == 0:
            terms = after(terms, *planes_got)
    scalars = (place, weights, traded_weights["A"], traded_weights["B"])
    enter, leave, zlow, zhigh = planes_got
    edge = shape(low_rows.shape, BF)
    for turn in range(PANELS - 1):
        from_panel = PANELS - 1 - turn
        target = from_panel - 1
        sums_now = cross(terms, from_panel, target)
        if turn < PANELS - 2:
            state, terms = backward_close(sums_now, (target,), target, True, "BA"[turn], state, brought)
        else:
            got_a, got_b = (swapped(state.astype(BF), which) for which in "AB")
            got = gather(sums_now, (target,), state)
            state, vectors, near_rows, far_rows = whole_call(
                functools.partial(closing_kernel, target),
                [shape(vector, F32), shape((two, 9, sources, width), F32), edge, edge], 300000000, "closing", 4,
                *scalars, *got, got_a, got_b, brought["A"], brought["B"], parcel,
                leaf_matrix, traded_leaf["A"], traded_leaf["B"], low_rows, high_rows, enter, leave, limit=32,
            )
    late = swapped(state, "A")
    near_front = other_core(near_rows)
    chain = [(p * FRONTS + f, p * FRONTS + (f + 1) % FRONTS) for p in range(PANELS) for f in range(1, FRONTS, 2)]
    far_front = moved(far_rows, pairing(chain))
    return tuple(
        finish(
            scalars, leaf, source, wave_term, vectors, late, enter, leave, near_front, far_front, zlow, zhigh
        )
    )


def solution(mesh):
    placed = (
        P(None, None, "panel", "front", None),
        P("panel", "front", None),
        P(None, "panel", "front", None, None),
        P(None, "panel", "front", None, None, None),
        P("panel", "front"),
        P("panel", "front"),
    )
    return jax.shard_map(
        local,
        mesh=mesh,
        in_specs=placed,
        out_specs=(P(None, None, "panel", "front", None), P(None, None, "panel", "front", None)),
        check_vma=False,
    )
```

```python
import functools

import jax
import jax.numpy as jnp
from jax import lax
from jax.experimental import pallas as pl
from jax.experimental.pallas import tpu as pltpu
from jax.sharding import PartitionSpec as P

DAMPING = 0.25
PANELS = 4
FRONTS = 32
AXES = ("panel", "front")
BF = jnp.bfloat16
F32 = jnp.float32
PAIRS = {"A": ((0, 1), (2, 3)), "B": ((1, 2), (0, 3))}


def pairing(swaps):
    target = {}
    for one, two in swaps:
        target[one] = two
        target[two] = one
    for device in range(PANELS * FRONTS):
        target.setdefault(device, device ^ 1)
    return sorted(target.items())


def within(panels, even, odd):
    swaps = []
    for panel in panels:
        for front in range(FRONTS):
            other = front ^ (odd if front % 2 else even)
            swaps.append((panel * FRONTS + front, panel * FRONTS + other))
    return pairing(swaps)


def across(pairs, even, odd):
    swaps = []
    for one, two in pairs:
        for front in range(FRONTS):
            other = front ^ (odd if front % 2 else even)
            swaps.append((one * FRONTS + front, two * FRONTS + other))
    return pairing(swaps)


def moved(block, route):
    return lax.ppermute(block, AXES, route)


def other_core(block):
    return moved(block, pairing(()))


def swapped(block, which):
    return moved(block, across(PAIRS[which], 0, 0))


def product(block, matrix_real, matrix_imag, half):
    by_real = jnp.dot(block, matrix_real, preferred_element_type=F32)
    by_imag = jnp.dot(block, matrix_imag, preferred_element_type=F32)
    return by_real[:half] - by_imag[half:], by_imag[:half] + by_real[half:]


def column(scalars, width):
    row = lax.broadcasted_iota(jnp.int32, (len(scalars), 128), 0)
    tile = jnp.full((len(scalars), 128), scalars[0])
    for i in range(1, len(scalars)):
        tile = jnp.where(row == i, scalars[i], tile)
    return jnp.concatenate([tile] * (width // 128), axis=1)


def dotted(one, two):
    total = one[0] * two[0]
    for a, b in zip(one[1:], two[1:]):
        total = total + a * b
    return total


def entries(ref, kind, plane):
    return [ref[kind, plane, x] for x in range(ref.shape[2])]


def leaf_kernel(weight_ref, source_ref, matrix_ref, leaf_ref, total_ref, first_ref, last_ref, low_ref, high_ref):
    count, planes, rows, width = source_ref.shape[1:]
    flat = count * planes * rows
    real = source_ref[0].reshape(flat, width).astype(BF)
    imag = source_ref[1].reshape(flat, width).astype(BF)
    dot = lambda a, b: jnp.dot(a, b, preferred_element_type=F32)
    out = (
        dot(real, matrix_ref[0]) - dot(imag, matrix_ref[1]),
        dot(real, matrix_ref[1]) + dot(imag, matrix_ref[0]),
    )
    columns = [column(entries(weight_ref, 0, z), width) for z in range(planes)]
    for part in range(2):
        shaped = out[part].reshape(count, planes, rows, width)
        leaf_ref[part] = shaped
        first_ref[part] = shaped[:, 0].astype(BF)
        last_ref[part] = shaped[:, planes - 1].astype(BF)
        low_ref[part] = shaped[:, :, 0]
        high_ref[part] = shaped[:, :, rows - 1]
        total = shaped[:, 0] * columns[0][None]
        for z in range(1, planes):
            total = total + shaped[:, z] * columns[z][None]
        total_ref[part] = jnp.sum(total, axis=1).astype(BF)


def leaf_solve(weights, source, matrix):
    two, sources, planes, rows, width = source.shape
    step = 8
    whole = pl.BlockSpec((two, step, planes, rows, width), lambda i: (0, i, 0, 0, 0))
    plane = pl.BlockSpec((two, step, rows, width), lambda i: (0, i, 0, 0))
    leaf, total, first, last, low, high = pl.pallas_call(
        leaf_kernel,
        grid=(sources // step,),
        in_specs=[
            pl.BlockSpec(memory_space=pltpu.SMEM),
            whole,
            pl.BlockSpec((two, width, width), lambda i: (0, 0, 0)),
        ],
        out_specs=[whole, pl.BlockSpec((two, step, width), lambda i: (0, i, 0)), plane, plane, plane, plane],
        out_shape=[
            pltpu.HBM(source.shape, F32),
            jax.ShapeDtypeStruct((two, sources, width), BF),
            jax.ShapeDtypeStruct((two, sources, rows, width), BF),
            jax.ShapeDtypeStruct((two, sources, rows, width), BF),
            pltpu.HBM((two, sources, planes, width), F32),
            pltpu.HBM((two, sources, planes, width), F32),
        ],
        compiler_params=pltpu.CompilerParams(vmem_limit_bytes=46 * 2**20),
        cost_estimate=pl.CostEstimate(flops=65000000, bytes_accessed=1600000, transcendentals=0),
        name="leaf_solve",
    )(weights, source, matrix)
    return leaf, total, first, last, low, high


def whole_call(kernel, shapes, cost, name, smem, *args, limit=14):
    spaces = [pltpu.SMEM] * smem + [pltpu.VMEM] * (len(args) - smem)
    return pl.pallas_call(
        kernel,
        in_specs=[pl.BlockSpec(memory_space=space) for space in spaces],
        out_specs=[pl.BlockSpec(memory_space=pltpu.VMEM)] * len(shapes),
        out_shape=shapes,
        compiler_params=pltpu.CompilerParams(vmem_limit_bytes=limit * 2**20),
        cost_estimate=pl.CostEstimate(flops=cost, bytes_accessed=cost // 200, transcendentals=0),
        name=name,
    )(*args)


def near_kernel(own_ref, quad_ref, slab_ref, matrix_ref, out_ref):
    sources, width = own_ref.shape[1:]
    total = None
    for level, ref in enumerate((own_ref, quad_ref, slab_ref)):
        block = ref[...].reshape(2 * sources, width).astype(BF)
        got = product(block, matrix_ref[0, level], matrix_ref[1, level], sources)
        total = got if total is None else (total[0] + got[0], total[1] + got[1])
    out_ref[0] = total[0]
    out_ref[1] = total[1]


def near_part(own, quad, slab, separators):
    return whole_call(
        near_kernel, [jax.ShapeDtypeStruct(own.shape, F32)], 150000000, "near_part", 0, own, quad, slab, separators
    )[0]


def advanced(target, keep, place_ref, near_ref, slab_ref, side_ref, opposite_ref, back_ref, before_ref, root_ref, state_ref):
    sources, width = near_ref.shape[1:]
    even = place_ref[0] == 1
    active = place_ref[1] == target
    mine = opposite_ref[...].astype(F32)
    other = back_ref[2].astype(F32)
    root = []
    for part in range(2):
        far = jnp.where(even, mine, other) if part == 0 else jnp.where(even, other, mine)
        root.append(slab_ref[part] + side_ref[part].astype(F32) + back_ref[part].astype(F32) + far)
    block = jnp.concatenate(root, axis=0).astype(BF)
    got = product(block, root_ref[0, 3], root_ref[1, 3], sources)
    state = []
    for part in range(2):
        old = before_ref[part]
        new = near_ref[part] + got[part]
        if keep:
            new = new + old
        state.append(jnp.where(active, new, old))
        state_ref[part] = state[part]
    return state, active


def forward_kernel(
    target, which, place_ref, own_ref, traded_ref, near_ref, slab_ref, side_ref, opposite_ref, back_ref, before_ref,
    root_ref, leaf_real_ref, leaf_imag_ref, sums_ref, parcel_ref, state_ref, terms_ref, out_ref,
):
    state, active = advanced(
        target, False, place_ref, near_ref, slab_ref, side_ref, opposite_ref, back_ref, before_ref, root_ref, state_ref
    )
    sources = near_ref.shape[1]
    end = own_ref.shape[1] - 1
    scale = dotted(entries(traded_ref, 0, 0), entries(own_ref, 1, end))
    own_scale = dotted(entries(own_ref, 0, end), entries(own_ref, 1, end))
    rows = []
    for part in range(2):
        here = state[part]
        rows += [sums_ref["AB".index(which), part] + scale * here, here, sums_ref[2, part] + own_scale * here]
    block = jnp.concatenate(rows, axis=0).astype(BF)
    got = product(block, leaf_real_ref[...], leaf_imag_ref[...], 3 * sources)
    for part in range(2):
        terms_ref[part] = got[part][:sources].astype(BF)
        for i in range(2):
            new = got[part][(i + 1) * sources : (i + 2) * sources].astype(BF)
            out_ref[i, part] = jnp.where(active, new, parcel_ref[i, part])


def backward_kernel(
    target, keep, which, place_ref, own_ref, traded_ref, near_ref, slab_ref, side_ref, opposite_ref, back_ref, before_ref,
    root_ref, leaf_real_ref, leaf_imag_ref, sums_ref, by_a_ref, by_b_ref, state_ref, terms_ref,
):
    state, _ = advanced(
        target, keep, place_ref, near_ref, slab_ref, side_ref, opposite_ref, back_ref, before_ref, root_ref, state_ref
    )
    sources = near_ref.shape[1]
    end = own_ref.shape[1] - 1
    even_panel = lax.rem(place_ref[1], 2) == 0
    scale = dotted(entries(traded_ref, 0, end), entries(own_ref, 1, 0))
    rows = []
    for part in range(2):
        echo = jnp.where(even_panel, by_b_ref[1, part], by_a_ref[1, part]).astype(F32)
        rows.append(sums_ref[3 + "AB".index(which), part] + echo + scale * state[part])
    block = jnp.concatenate(rows, axis=0).astype(BF)
    got = product(block, leaf_real_ref[...], leaf_imag_ref[...], sources)
    for part in range(2):
        terms_ref[part] = got[part].astype(BF)


def sums_kernel(own_ref, by_a_ref, by_b_ref, first_ref, last_ref, out_ref):
    width = first_ref.shape[3]
    end = own_ref.shape[1] - 1
    tables = [
        (last_ref, column(entries(by_a_ref, 0, 0), width)),
        (last_ref, column(entries(by_b_ref, 0, 0), width)),
        (last_ref, column(entries(own_ref, 0, end), width)),
        (first_ref, column(entries(by_a_ref, 0, end), width)),
        (first_ref, column(entries(by_b_ref, 0, end), width)),
    ]
    for part in range(2):
        for i, (ref, table) in enumerate(tables):
            out_ref[i, part] = jnp.sum(ref[part].astype(F32) * table[None], axis=1)


def planes_kernel(
    place_ref, by_a_ref, by_b_ref, first_ref, last_ref, own_ref, a_real_ref, a_imag_ref, b_real_ref, b_imag_ref,
    enter_ref, leave_ref, zlow_ref, zhigh_ref,
):
    two, sources, rows, width = first_ref.shape
    flat = sources * rows
    panel = place_ref[1]
    even = lax.rem(panel, 2) == 0
    lower = panel > 0
    upper = panel < PANELS - 1

    def stacked(parts):
        return jnp.concatenate([part.reshape(flat, width) for part in parts], axis=0).astype(BF)

    def times(parts, matrix):
        return [part.reshape(sources, rows, width) for part in product(stacked(parts), matrix[0], matrix[1], flat)]

    below = [jnp.where(even, by_b_ref[part], by_a_ref[part]).astype(F32) for part in range(2)]
    below = [jnp.where(lower, part, 0.0) for part in below]
    above = [jnp.where(even, by_a_ref[part], by_b_ref[part]).astype(F32) for part in range(2)]
    leaf_a, leaf_b = (a_real_ref[...], a_imag_ref[...]), (b_real_ref[...], b_imag_ref[...])
    upper_leaf = [jnp.where(even, leaf_a[part], leaf_b[part]) for part in range(2)]
    lower_leaf = [jnp.where(even, leaf_b[part], leaf_a[part]) for part in range(2)]
    own_leaf = [own_ref[0], own_ref[1]]
    enter = times(below, own_leaf)
    above_enter = times([last_ref[part].astype(F32) for part in range(2)], upper_leaf)
    zhigh = [jnp.where(upper, above[part] + above_enter[part], 0.0) for part in range(2)]
    leave = times(zhigh, own_leaf)
    below_leave = times([first_ref[part].astype(F32) + enter[part] for part in range(2)], lower_leaf)
    for part in range(2):
        enter_ref[part] = enter[part]
        leave_ref[part] = leave[part]
        zhigh_ref[part] = zhigh[part]
        zlow_ref[part] = jnp.where(lower, below[part] + below_leave[part], 0.0)


def neighbour_tables(place_ref, by_a_ref, by_b_ref, end):
    panel = place_ref[1]
    even = lax.rem(panel, 2) == 0
    pick = lambda one, two, there: jnp.where(there, jnp.where(even, one, two), 0.0)
    below = [
        pick(b, a, panel > 0) for a, b in zip(entries(by_a_ref, 1, end), entries(by_b_ref, 1, end))
    ]
    above = [
        pick(a, b, panel < PANELS - 1) for a, b in zip(entries(by_a_ref, 1, 0), entries(by_b_ref, 1, 0))
    ]
    return below, above


def closing_kernel(
    target, place_ref, own_w_ref, a_w_ref, b_w_ref, near_ref, slab_ref, side_ref, opposite_ref, back_ref, before_ref,
    root_ref, got_a_ref, got_b_ref, parcel_a_ref, parcel_b_ref, parcel_ref, own_ref, a_real_ref, a_imag_ref, b_real_ref, b_imag_ref,
    low_ref, high_ref, enter_ref, leave_ref, state_ref, vector_ref, near_rows_ref, far_rows_ref,
):
    here, _ = advanced(
        target, True, place_ref, near_ref, slab_ref, side_ref, opposite_ref, back_ref, before_ref, root_ref, state_ref
    )
    sources, planes, width = low_ref.shape[1:]
    rows = enter_ref.shape[2]
    panel = place_ref[1]
    even_core = place_ref[0] == 1
    even = lax.rem(panel, 2) == 0
    lower = panel > 0
    upper = panel < PANELS - 1
    below_last, above_first = neighbour_tables(place_ref, a_w_ref, b_w_ref, planes - 1)
    own_last = entries(own_w_ref, 1, planes - 1)
    own_leaf = [own_ref[0], own_ref[1]]
    lower_leaf = [jnp.where(even, b, a) for a, b in ((a_real_ref[...], b_real_ref[...]), (a_imag_ref[...], b_imag_ref[...]))]
    entered, above, below, behind = [], [], [], []
    for part in range(2):
        entered.append(jnp.where(lower, jnp.where(even, parcel_b_ref[0, part], parcel_a_ref[0, part]).astype(F32), 0.0))
        above.append(jnp.where(even, got_a_ref[part], got_b_ref[part]).astype(F32))
        below.append(jnp.where(even, got_b_ref[part], got_a_ref[part]).astype(F32))
        behind.append(jnp.where(upper, parcel_ref[0, part].astype(F32), 0.0))
    stacked = lambda one, two: jnp.concatenate([one[0], two[0], one[1], two[1]], axis=0).astype(BF)
    out_up = product(stacked(above, behind), own_leaf[0], own_leaf[1], 2 * sources)
    out_down = product(stacked(here, entered), lower_leaf[0], lower_leaf[1], 2 * sources)
    depth = lax.broadcasted_iota(jnp.int32, (planes, width), 0)
    ends = [column([own_w_ref[1, z, x] for z in range(planes)], width) for x in (0, rows - 1)]
    for part in range(2):
        down = jnp.where(lower, out_down[part], 0.0)
        vectors = [
            here[part], entered[part], above[part], below[part], behind[part],
            out_up[part][:sources], out_up[part][sources:], down[:sources], down[sources:],
        ]
        for i, vector in enumerate(vectors):
            vector_ref[part, i] = vector
        for b in range(sources):
            row = lambda i: vector_ref[part, i, b : b + 1]
            done = []
            for side, ref in ((0, low_ref), (1, high_ref)):
                x = 0 if side == 0 else rows - 1
                enter = enter_ref[part, b, x : x + 1] + below_last[x] * row(1)
                leave = leave_ref[part, b, x : x + 1] + above_first[x] * row(5) + own_last[x] * row(6)
                tile = ref[part, b] + ends[side] * row(0)
                tile = tile + jnp.where(depth == 0, enter, 0.0) + jnp.where(depth == planes - 1, leave, 0.0)
                done.append(tile)
            near_rows_ref[part, b] = jnp.where(even_core, done[1], done[0]).astype(BF)
            far_rows_ref[part, b] = jnp.where(even_core, done[0], done[1]).astype(BF)


def final_kernel(
    place_ref, own_w_ref, a_w_ref, b_w_ref, leaf_ref, source_ref, wave_ref, vector_ref, late_ref, enter_ref, leave_ref,
    near_ref, far_ref, zlow_ref, zhigh_ref, field_ref, residual_ref,
):
    count, planes, rows, width = leaf_ref.shape[1:]
    lane = lax.broadcasted_iota(jnp.int32, (rows, width), 1)
    row = lax.broadcasted_iota(jnp.int32, (rows, width), 0)
    even_core = place_ref[0] == 1
    low_there = place_ref[2] > 0
    high_there = place_ref[2] < FRONTS - 1
    below_last, above_first = (
        column(table, width) for table in neighbour_tables(place_ref, a_w_ref, b_w_ref, planes - 1)
    )
    prolong = [column(entries(own_w_ref, 1, z), width) for z in range(planes)]
    own_last, own_first = prolong[planes - 1], prolong[0]
    even = lax.rem(place_ref[1], 2) == 0
    start = pl.program_id(0) * count
    for b in range(count):
        at = start + b
        field, ends = [], []
        for part in range(2):
            vec = [vector_ref[part, i, pl.ds(at, 1)] for i in range(9)]
            lower = jnp.where(even, vec[3], late_ref[part, pl.ds(at, 1)])
            tiles = []
            for z in range(planes):
                tile = leaf_ref[part, b, z] + prolong[z] * vec[0]
                if z == 0:
                    tile = tile + enter_ref[part, at] + below_last * vec[1]
                if z == planes - 1:
                    tile = tile + leave_ref[part, at] + above_first * vec[5] + own_last * vec[6]
                field_ref[part, b, z] = tile
                tiles.append(tile)
            field.append(tiles)
            below = zlow_ref[part, at] + below_last * (lower + vec[8]) + own_first * vec[7]
            above = zhigh_ref[part, at] + above_first * vec[2] + own_last * vec[4]
            ends.append((below, above))
        for part in range(2):
            tiles = field[part]
            near_rows = near_ref[part, at].astype(F32)
            far_rows = far_ref[part, at].astype(F32)
            low_rows = jnp.where(even_core, jnp.where(low_there, far_rows, 0.0), near_rows)
            high_rows = jnp.where(even_core, near_rows, jnp.where(high_there, far_rows, 0.0))
            for z in range(planes):
                diag_real = 6.0 - wave_ref[z]
                diag_imag = -DAMPING * wave_ref[z]
                here = tiles[z]
                below = tiles[z - 1] if z else ends[part][0]
                above = tiles[z + 1] if z < planes - 1 else ends[part][1]
                near = below + above
                low = jnp.where(row == 0, low_rows[z : z + 1], pltpu.roll(here, 1, 0))
                high = jnp.where(row == rows - 1, high_rows[z : z + 1], pltpu.roll(here, rows - 1, 0))
                near = near + low + high
                left = jnp.where(lane == 0, 0.0, pltpu.roll(here, 1, 1))
                right = jnp.where(lane == width - 1, 0.0, pltpu.roll(here, width - 1, 1))
                near = near + left + right
                cross = diag_imag * field[1 - part][z]
                applied = diag_real * here - near
                applied = applied - cross if part == 0 else applied + cross
                residual_ref[part, b, z] = source_ref[part, b, z] - applied


def finish(scalars, leaf, source, *others):
    two, sources, planes, rows, width = source.shape
    step = 4
    whole = pl.BlockSpec((two, step, planes, rows, width), lambda i: (0, i, 0, 0, 0))
    return pl.pallas_call(
        final_kernel,
        grid=(sources // step,),
        in_specs=[pl.BlockSpec(memory_space=pltpu.SMEM)] * len(scalars)
        + [whole, whole]
        + [pl.BlockSpec(memory_space=pltpu.VMEM)] * len(others),
        out_specs=[whole, whole],
        out_shape=[jax.ShapeDtypeStruct(source.shape, F32)] * 2,
        compiler_params=pltpu.CompilerParams(vmem_limit_bytes=46 * 2**20),
        cost_estimate=pl.CostEstimate(flops=60000000, bytes_accessed=26000000, transcendentals=0),
        name="finish",
    )(*scalars, leaf, source, *others)


def after(value, *others):
    return lax.optimization_barrier((value, *others))[0]


def local(source, wave_term, leaf_inverse, separator_inverse, restrict_weight, prolong_weight):
    two, sources, planes, rows, width = source.shape
    panel = lax.axis_index("panel")
    front = lax.axis_index("front")
    even_core = front % 2 == 0
    even_panel = panel % 2 == 0
    leaf_matrix = leaf_inverse[:, 0, 0]
    separators = separator_inverse[:, 0, 0]
    place = jnp.stack([even_core.astype(jnp.int32), panel, front])
    vector = (two, sources, width)
    shape = jax.ShapeDtypeStruct

    weights = jnp.stack([restrict_weight, prolong_weight])
    traded_leaf = {which: [swapped(leaf_matrix[part], which) for part in range(2)] for which in "AB"}
    real_parts, imag_parts = zip(*traded_leaf.values())
    leaf, base_terms, first_plane, last_plane, low_rows, high_rows = leaf_solve(weights, source, leaf_matrix)


    def halves(block):
        return jnp.where(even_core, block[0], block[1])

    def inside(sent, panels, near, far, cross):
        side = moved(sent, within(panels, near, cross))
        opposite = moved(halves(sent), within(panels, far, far))
        back = other_core(jnp.concatenate([side, opposite[None]]))
        return side, opposite, back

    def pair_sum(terms):
        return terms.astype(F32) + other_core(terms).astype(F32)

    every = tuple(range(PANELS))
    pair = after(pair_sum(base_terms), *real_parts)
    side, opposite, back = inside(pair.astype(BF), every, 2, 4, 6)
    near_term = jnp.where(even_core, side, back[:2]).astype(F32)
    far_term = jnp.where(even_core, jnp.stack([opposite, back[2]]), jnp.stack([back[2], opposite])).astype(F32)
    quad = pair + near_term
    slab = pair + side.astype(F32) + back[:2].astype(F32) + far_term
    slab = after(slab, *imag_parts)
    traded_weights = {which: swapped(after(weights, slab), which) for which in "AB"}
    def by_parity(even_value, odd_value):
        return jnp.where(even_panel, even_value, odd_value)

    by_a = swapped(after(by_parity(last_plane, first_plane), slab), "A")
    by_b = swapped(after(by_parity(first_plane, last_plane), slab), "B")
    plane = shape(first_plane.shape, F32)
    planes_got = whole_call(
        planes_kernel, [plane] * 4, 400000000, "planes", 1,
        place, by_a, by_b, first_plane, last_plane, leaf_matrix, *traded_leaf["A"], *traded_leaf["B"], limit=26,
    )
    base_sums = (pair, quad, slab)
    nothing = jnp.zeros(vector, F32)

    sums = whole_call(
        sums_kernel, [shape((5,) + vector, F32)], 10000000, "edge_sums", 3,
        weights, traded_weights["A"], traded_weights["B"], first_plane, last_plane,
    )[0]

    def gather(level_sums, panels, before):
        own, quad, slab = level_sums
        near = near_part(own, quad, slab, separators)
        return (near, slab, *inside(slab.astype(BF), panels, 8, 16, 24), before, separators)

    def forward_close(level_sums, panels, target, which, before, parcel):
        got = gather(level_sums, panels, before)
        return whole_call(
            functools.partial(forward_kernel, target, which),
            [shape(vector, F32), shape(vector, BF), shape((2,) + vector, BF)], 200000000, "forward", 3,
            place, weights, traded_weights[which], *got, *traded_leaf[which], sums, parcel,
        )

    def backward_close(level_sums, panels, target, keep, which, before, brought):
        got = gather(level_sums, panels, before)
        return whole_call(
            functools.partial(backward_kernel, target, keep, which),
            [shape(vector, F32), shape(vector, BF)], 200000000, "backward", 3,
            place, weights, traded_weights[which], *got, *traded_leaf[which], sums, brought["A"], brought["B"],
        )

    def cross(terms, from_panel, to_panel):
        sent = pair_sum(terms).astype(BF)
        ends = ((from_panel, to_panel),)
        one = moved(sent, across(ends, 0, 2))
        two_ = moved(sent, across(ends, 4, 6))
        back = other_core(jnp.stack([one, two_])).astype(F32)
        one = one.astype(F32)
        own = jnp.where(even_core, one, back[0])
        quad = one + back[0]
        return own, quad, quad + two_.astype(F32) + back[1]

    state, terms, parcel = forward_close(base_sums, every, 0, "A", nothing, jnp.zeros((2,) + vector, BF))
    terms = after(terms, by_a, by_b)
    brought = {}
    for turn, which in enumerate("ABA"):
        target = turn + 1
        sums_now = cross(terms, turn, target)
        if turn > 0:
            brought[which] = swapped(parcel, which)
        total = tuple(a + b for a, b in zip(sums_now, base_sums))
        if turn < 2:
            state, terms, parcel = forward_close(total, (target,), target, "BA"[turn], state, parcel)
        else:
            state, terms = backward_close(total, (target,), target, False, "A", state, brought)
        if turn == 0:
            terms = after(terms, *planes_got)
    scalars = (place, weights, traded_weights["A"], traded_weights["B"])
    enter, leave, zlow, zhigh = planes_got
    edge = shape(low_rows.shape, BF)
    for turn in range(PANELS - 1):
        from_panel = PANELS - 1 - turn
        target = from_panel - 1
        sums_now = cross(terms, from_panel, target)
        if turn < PANELS - 2:
            state, terms = backward_close(sums_now, (target,), target, True, "BA"[turn], state, brought)
        else:
            got_a, got_b = (swapped(state.astype(BF), which) for which in "AB")
            got = gather(sums_now, (target,), state)
            state, vectors, near_rows, far_rows = whole_call(
                functools.partial(closing_kernel, target),
                [shape(vector, F32), shape((two, 9, sources, width), F32), edge, edge], 300000000, "closing", 4,
                *scalars, *got, got_a, got_b, brought["A"], brought["B"], parcel,
                leaf_matrix, *traded_leaf["A"], *traded_leaf["B"], low_rows, high_rows, enter, leave, limit=26,
            )
    late = swapped(state, "A")
    near_front = other_core(near_rows)
    chain = [(p * FRONTS + f, p * FRONTS + (f + 1) % FRONTS) for p in range(PANELS) for f in range(1, FRONTS, 2)]
    far_front = moved(far_rows, pairing(chain))
    return tuple(
        finish(
            scalars, leaf, source, wave_term, vectors, late, enter, leave, near_front, far_front, zlow, zhigh
        )
    )


def solution(mesh):
    placed = (
        P(None, None, "panel", "front", None),
        P("panel", "front", None),
        P(None, "panel", "front", None, None),
        P(None, "panel", "front", None, None, None),
        P("panel", "front"),
        P("panel", "front"),
    )
    return jax.shard_map(
        local,
        mesh=mesh,
        in_specs=placed,
        out_specs=(P(None, None, "panel", "front", None), P(None, None, "panel", "front", None)),
        check_vma=False,
    )
```

```python
import functools

import jax
import jax.numpy as jnp
from jax import lax
from jax.experimental import pallas as pl
from jax.experimental.pallas import tpu as pltpu
from jax.sharding import PartitionSpec as P

DAMPING = 0.25
PANELS = 4
FRONTS = 32
AXES = ("panel", "front")
BF = jnp.bfloat16
F32 = jnp.float32
PAIRS = {"A": ((0, 1), (2, 3)), "B": ((1, 2), (0, 3))}


def pairing(swaps):
    target = {}
    for one, two in swaps:
        target[one] = two
        target[two] = one
    for device in range(PANELS * FRONTS):
        target.setdefault(device, device ^ 1)
    return sorted(target.items())


def within(panels, even, odd):
    swaps = []
    for panel in panels:
        for front in range(FRONTS):
            other = front ^ (odd if front % 2 else even)
            swaps.append((panel * FRONTS + front, panel * FRONTS + other))
    return pairing(swaps)


def across(pairs, even, odd):
    swaps = []
    for one, two in pairs:
        for front in range(FRONTS):
            other = front ^ (odd if front % 2 else even)
            swaps.append((one * FRONTS + front, two * FRONTS + other))
    return pairing(swaps)


def moved(block, route):
    return lax.ppermute(block, AXES, route)


def other_core(block):
    return moved(block, pairing(()))


def swapped(block, which):
    return moved(block, across(PAIRS[which], 0, 0))


def product(block, matrix_real, matrix_imag, half):
    by_real = jnp.dot(block, matrix_real, preferred_element_type=F32)
    by_imag = jnp.dot(block, matrix_imag, preferred_element_type=F32)
    return by_real[:half] - by_imag[half:], by_imag[:half] + by_real[half:]


def column(scalars, width):
    row = lax.broadcasted_iota(jnp.int32, (len(scalars), 128), 0)
    tile = jnp.full((len(scalars), 128), scalars[0])
    for i in range(1, len(scalars)):
        tile = jnp.where(row == i, scalars[i], tile)
    return jnp.concatenate([tile] * (width // 128), axis=1)


def dotted(one, two):
    total = one[0] * two[0]
    for a, b in zip(one[1:], two[1:]):
        total = total + a * b
    return total


def entries(ref, kind, plane):
    return [ref[kind, plane, x] for x in range(ref.shape[2])]


def leaf_kernel(weight_ref, source_ref, matrix_ref, leaf_ref, total_ref, first_ref, last_ref, low_ref, high_ref):
    count, planes, rows, width = source_ref.shape[1:]
    flat = count * planes * rows
    real = source_ref[0].reshape(flat, width).astype(BF)
    imag = source_ref[1].reshape(flat, width).astype(BF)
    dot = lambda a, b: jnp.dot(a, b, preferred_element_type=F32)
    out = (
        dot(real, matrix_ref[0]) - dot(imag, matrix_ref[1]),
        dot(real, matrix_ref[1]) + dot(imag, matrix_ref[0]),
    )
    columns = [column(entries(weight_ref, 0, z), width) for z in range(planes)]
    for part in range(2):
        shaped = out[part].reshape(count, planes, rows, width)
        leaf_ref[part] = shaped
        first_ref[part] = shaped[:, 0].astype(BF)
        last_ref[part] = shaped[:, planes - 1].astype(BF)
        low_ref[part] = shaped[:, :, 0]
        high_ref[part] = shaped[:, :, rows - 1]
        total = shaped[:, 0] * columns[0][None]
        for z in range(1, planes):
            total = total + shaped[:, z] * columns[z][None]
        total_ref[part] = jnp.sum(total, axis=1).astype(BF)


def leaf_solve(weights, source, matrix):
    two, sources, planes, rows, width = source.shape
    step = 8
    whole = pl.BlockSpec((two, step, planes, rows, width), lambda i: (0, i, 0, 0, 0))
    plane = pl.BlockSpec((two, step, rows, width), lambda i: (0, i, 0, 0))
    leaf, total, first, last, low, high = pl.pallas_call(
        leaf_kernel,
        grid=(sources // step,),
        in_specs=[
            pl.BlockSpec(memory_space=pltpu.SMEM),
            whole,
            pl.BlockSpec((two, width, width), lambda i: (0, 0, 0)),
        ],
        out_specs=[whole, pl.BlockSpec((two, step, width), lambda i: (0, i, 0)), plane, plane, plane, plane],
        out_shape=[
            pltpu.HBM(source.shape, F32),
            jax.ShapeDtypeStruct((two, sources, width), BF),
            jax.ShapeDtypeStruct((two, sources, rows, width), BF),
            jax.ShapeDtypeStruct((two, sources, rows, width), BF),
            pltpu.HBM((two, sources, planes, width), F32),
            pltpu.HBM((two, sources, planes, width), F32),
        ],
        compiler_params=pltpu.CompilerParams(vmem_limit_bytes=40 * 2**20),
        cost_estimate=pl.CostEstimate(flops=65000000, bytes_accessed=1600000, transcendentals=0),
        name="leaf_solve",
    )(weights, source, matrix)
    return leaf, total, first, last, low, high


def whole_call(kernel, shapes, cost, name, smem, *args, limit=14):
    spaces = [pltpu.SMEM] * smem + [pltpu.VMEM] * (len(args) - smem)
    return pl.pallas_call(
        kernel,
        in_specs=[pl.BlockSpec(memory_space=space) for space in spaces],
        out_specs=[pl.BlockSpec(memory_space=pltpu.VMEM)] * len(shapes),
        out_shape=shapes,
        compiler_params=pltpu.CompilerParams(vmem_limit_bytes=limit * 2**20),
        cost_estimate=pl.CostEstimate(flops=cost, bytes_accessed=cost // 200, transcendentals=0),
        name=name,
    )(*args)


def near_kernel(own_ref, quad_ref, slab_ref, matrix_ref, out_ref):
    sources, width = own_ref.shape[1:]
    total = None
    for level, ref in enumerate((own_ref, quad_ref, slab_ref)):
        block = ref[...].reshape(2 * sources, width).astype(BF)
        got = product(block, matrix_ref[0, level], matrix_ref[1, level], sources)
        total = got if total is None else (total[0] + got[0], total[1] + got[1])
    out_ref[0] = total[0]
    out_ref[1] = total[1]


def near_part(own, quad, slab, separators):
    return whole_call(
        near_kernel, [jax.ShapeDtypeStruct(own.shape, F32)], 150000000, "near_part", 0, own, quad, slab, separators
    )[0]


def advanced(target, keep, place_ref, near_ref, slab_ref, side_ref, opposite_ref, back_ref, before_ref, root_ref, state_ref):
    sources, width = near_ref.shape[1:]
    even = place_ref[0] == 1
    active = place_ref[1] == target
    mine = opposite_ref[...].astype(F32)
    other = back_ref[2].astype(F32)
    root = []
    for part in range(2):
        far = jnp.where(even, mine, other) if part == 0 else jnp.where(even, other, mine)
        root.append(slab_ref[part] + side_ref[part].astype(F32) + back_ref[part].astype(F32) + far)
    block = jnp.concatenate(root, axis=0).astype(BF)
    got = product(block, root_ref[0, 3], root_ref[1, 3], sources)
    state = []
    for part in range(2):
        old = before_ref[part]
        new = near_ref[part] + got[part]
        if keep:
            new = new + old
        state.append(jnp.where(active, new, old))
        state_ref[part] = state[part]
    return state, active


def forward_kernel(
    target, which, place_ref, own_ref, traded_ref, near_ref, slab_ref, side_ref, opposite_ref, back_ref, before_ref,
    root_ref, leaf_real_ref, leaf_imag_ref, sums_ref, parcel_ref, state_ref, terms_ref, out_ref,
):
    state, active = advanced(
        target, False, place_ref, near_ref, slab_ref, side_ref, opposite_ref, back_ref, before_ref, root_ref, state_ref
    )
    sources = near_ref.shape[1]
    end = own_ref.shape[1] - 1
    scale = dotted(entries(traded_ref, 0, 0), entries(own_ref, 1, end))
    own_scale = dotted(entries(own_ref, 0, end), entries(own_ref, 1, end))
    rows = []
    for part in range(2):
        here = state[part]
        rows += [sums_ref["AB".index(which), part] + scale * here, here, sums_ref[2, part] + own_scale * here]
    block = jnp.concatenate(rows, axis=0).astype(BF)
    got = product(block, leaf_real_ref[...], leaf_imag_ref[...], 3 * sources)
    for part in range(2):
        terms_ref[part] = got[part][:sources].astype(BF)
        for i in range(2):
            new = got[part][(i + 1) * sources : (i + 2) * sources].astype(BF)
            out_ref[i, part] = jnp.where(active, new, parcel_ref[i, part])


def backward_kernel(
    target, keep, which, place_ref, own_ref, traded_ref, near_ref, slab_ref, side_ref, opposite_ref, back_ref, before_ref,
    root_ref, leaf_real_ref, leaf_imag_ref, sums_ref, by_a_ref, by_b_ref, state_ref, terms_ref,
):
    state, _ = advanced(
        target, keep, place_ref, near_ref, slab_ref, side_ref, opposite_ref, back_ref, before_ref, root_ref, state_ref
    )
    sources = near_ref.shape[1]
    end = own_ref.shape[1] - 1
    even_panel = lax.rem(place_ref[1], 2) == 0
    scale = dotted(entries(traded_ref, 0, end), entries(own_ref, 1, 0))
    rows = []
    for part in range(2):
        echo = jnp.where(even_panel, by_b_ref[1, part], by_a_ref[1, part]).astype(F32)
        rows.append(sums_ref[3 + "AB".index(which), part] + echo + scale * state[part])
    block = jnp.concatenate(rows, axis=0).astype(BF)
    got = product(block, leaf_real_ref[...], leaf_imag_ref[...], sources)
    for part in range(2):
        terms_ref[part] = got[part].astype(BF)


def sums_kernel(own_ref, by_a_ref, by_b_ref, first_ref, last_ref, out_ref):
    width = first_ref.shape[3]
    end = own_ref.shape[1] - 1
    tables = [
        (last_ref, column(entries(by_a_ref, 0, 0), width)),
        (last_ref, column(entries(by_b_ref, 0, 0), width)),
        (last_ref, column(entries(own_ref, 0, end), width)),
        (first_ref, column(entries(by_a_ref, 0, end), width)),
        (first_ref, column(entries(by_b_ref, 0, end), width)),
    ]
    for part in range(2):
        for i, (ref, table) in enumerate(tables):
            out_ref[i, part] = jnp.sum(ref[part].astype(F32) * table[None], axis=1)


def planes_kernel(
    place_ref, by_a_ref, by_b_ref, first_ref, last_ref, own_ref, a_real_ref, a_imag_ref, b_real_ref, b_imag_ref,
    enter_ref, leave_ref, zlow_ref, zhigh_ref,
):
    two, sources, rows, width = first_ref.shape
    flat = sources * rows
    panel = place_ref[1]
    even = lax.rem(panel, 2) == 0
    lower = panel > 0
    upper = panel < PANELS - 1

    def stacked(parts):
        return jnp.concatenate([part.reshape(flat, width) for part in parts], axis=0).astype(BF)

    def times(parts, matrix):
        return [part.reshape(sources, rows, width) for part in product(stacked(parts), matrix[0], matrix[1], flat)]

    below = [jnp.where(even, by_b_ref[part], by_a_ref[part]).astype(F32) for part in range(2)]
    below = [jnp.where(lower, part, 0.0) for part in below]
    above = [jnp.where(even, by_a_ref[part], by_b_ref[part]).astype(F32) for part in range(2)]
    leaf_a, leaf_b = (a_real_ref[...], a_imag_ref[...]), (b_real_ref[...], b_imag_ref[...])
    upper_leaf = [jnp.where(even, leaf_a[part], leaf_b[part]) for part in range(2)]
    lower_leaf = [jnp.where(even, leaf_b[part], leaf_a[part]) for part in range(2)]
    own_leaf = [own_ref[0], own_ref[1]]
    enter = times(below, own_leaf)
    above_enter = times([last_ref[part].astype(F32) for part in range(2)], upper_leaf)
    zhigh = [jnp.where(upper, above[part] + above_enter[part], 0.0) for part in range(2)]
    leave = times(zhigh, own_leaf)
    below_leave = times([first_ref[part].astype(F32) + enter[part] for part in range(2)], lower_leaf)
    for part in range(2):
        enter_ref[part] = enter[part]
        leave_ref[part] = leave[part]
        zhigh_ref[part] = zhigh[part]
        zlow_ref[part] = jnp.where(lower, below[part] + below_leave[part], 0.0)


def neighbour_tables(place_ref, by_a_ref, by_b_ref, end):
    panel = place_ref[1]
    even = lax.rem(panel, 2) == 0
    pick = lambda one, two, there: jnp.where(there, jnp.where(even, one, two), 0.0)
    below = [
        pick(b, a, panel > 0) for a, b in zip(entries(by_a_ref, 1, end), entries(by_b_ref, 1, end))
    ]
    above = [
        pick(a, b, panel < PANELS - 1) for a, b in zip(entries(by_a_ref, 1, 0), entries(by_b_ref, 1, 0))
    ]
    return below, above


def closing_kernel(
    target, place_ref, own_w_ref, a_w_ref, b_w_ref, near_ref, slab_ref, side_ref, opposite_ref, back_ref, before_ref,
    root_ref, got_a_ref, got_b_ref, parcel_a_ref, parcel_b_ref, parcel_ref, own_ref, a_real_ref, a_imag_ref, b_real_ref, b_imag_ref,
    low_ref, high_ref, enter_ref, leave_ref, state_ref, vector_ref, near_rows_ref, far_rows_ref,
):
    here, _ = advanced(
        target, True, place_ref, near_ref, slab_ref, side_ref, opposite_ref, back_ref, before_ref, root_ref, state_ref
    )
    sources, planes, width = low_ref.shape[1:]
    rows = enter_ref.shape[2]
    panel = place_ref[1]
    even_core = place_ref[0] == 1
    even = lax.rem(panel, 2) == 0
    lower = panel > 0
    upper = panel < PANELS - 1
    below_last, above_first = neighbour_tables(place_ref, a_w_ref, b_w_ref, planes - 1)
    own_last = entries(own_w_ref, 1, planes - 1)
    own_leaf = [own_ref[0], own_ref[1]]
    lower_leaf = [jnp.where(even, b, a) for a, b in ((a_real_ref[...], b_real_ref[...]), (a_imag_ref[...], b_imag_ref[...]))]
    entered, above, below, behind = [], [], [], []
    for part in range(2):
        entered.append(jnp.where(lower, jnp.where(even, parcel_b_ref[0, part], parcel_a_ref[0, part]).astype(F32), 0.0))
        above.append(jnp.where(even, got_a_ref[part], got_b_ref[part]).astype(F32))
        below.append(jnp.where(even, got_b_ref[part], got_a_ref[part]).astype(F32))
        behind.append(jnp.where(upper, parcel_ref[0, part].astype(F32), 0.0))
    stacked = lambda one, two: jnp.concatenate([one[0], two[0], one[1], two[1]], axis=0).astype(BF)
    out_up = product(stacked(above, behind), own_leaf[0], own_leaf[1], 2 * sources)
    out_down = product(stacked(here, entered), lower_leaf[0], lower_leaf[1], 2 * sources)
    depth = lax.broadcasted_iota(jnp.int32, (planes, width), 0)
    ends = [column([own_w_ref[1, z, x] for z in range(planes)], width) for x in (0, rows - 1)]
    for part in range(2):
        down = jnp.where(lower, out_down[part], 0.0)
        vectors = [
            here[part], entered[part], above[part], below[part], behind[part],
            out_up[part][:sources], out_up[part][sources:], down[:sources], down[sources:],
        ]
        for i, vector in enumerate(vectors):
            vector_ref[part, i] = vector
        for b in range(sources):
            row = lambda i: vector_ref[part, i, b : b + 1]
            done = []
            for side, ref in ((0, low_ref), (1, high_ref)):
                x = 0 if side == 0 else rows - 1
                enter = enter_ref[part, b, x : x + 1] + below_last[x] * row(1)
                leave = leave_ref[part, b, x : x + 1] + above_first[x] * row(5) + own_last[x] * row(6)
                tile = ref[part, b] + ends[side] * row(0)
                tile = tile + jnp.where(depth == 0, enter, 0.0) + jnp.where(depth == planes - 1, leave, 0.0)
                done.append(tile)
            near_rows_ref[part, b] = jnp.where(even_core, done[1], done[0]).astype(BF)
            far_rows_ref[part, b] = jnp.where(even_core, done[0], done[1]).astype(BF)


def final_kernel(
    place_ref, own_w_ref, a_w_ref, b_w_ref, leaf_ref, source_ref, wave_ref, vector_ref, late_ref, enter_ref, leave_ref,
    near_ref, far_ref, zlow_ref, zhigh_ref, field_ref, residual_ref,
):
    count, planes, rows, width = leaf_ref.shape[1:]
    lane = lax.broadcasted_iota(jnp.int32, (rows, width), 1)
    row = lax.broadcasted_iota(jnp.int32, (rows, width), 0)
    even_core = place_ref[0] == 1
    low_there = place_ref[2] > 0
    high_there = place_ref[2] < FRONTS - 1
    below_last, above_first = (
        column(table, width) for table in neighbour_tables(place_ref, a_w_ref, b_w_ref, planes - 1)
    )
    prolong = [column(entries(own_w_ref, 1, z), width) for z in range(planes)]
    own_last, own_first = prolong[planes - 1], prolong[0]
    even = lax.rem(place_ref[1], 2) == 0
    start = pl.program_id(0) * count
    for b in range(count):
        at = start + b
        field, ends = [], []
        for part in range(2):
            vec = [vector_ref[part, i, pl.ds(at, 1)] for i in range(9)]
            lower = jnp.where(even, vec[3], late_ref[part, pl.ds(at, 1)])
            tiles = []
            for z in range(planes):
                tile = leaf_ref[part, b, z] + prolong[z] * vec[0]
                if z == 0:
                    tile = tile + enter_ref[part, at] + below_last * vec[1]
                if z == planes - 1:
                    tile = tile + leave_ref[part, at] + above_first * vec[5] + own_last * vec[6]
                field_ref[part, b, z] = tile
                tiles.append(tile)
            field.append(tiles)
            below = zlow_ref[part, at] + below_last * (lower + vec[8]) + own_first * vec[7]
            above = zhigh_ref[part, at] + above_first * vec[2] + own_last * vec[4]
            ends.append((below, above))
        for part in range(2):
            tiles = field[part]
            near_rows = near_ref[part, at].astype(F32)
            far_rows = far_ref[part, at].astype(F32)
            low_rows = jnp.where(even_core, jnp.where(low_there, far_rows, 0.0), near_rows)
            high_rows = jnp.where(even_core, near_rows, jnp.where(high_there, far_rows, 0.0))
            for z in range(planes):
                diag_real = 6.0 - wave_ref[z]
                diag_imag = -DAMPING * wave_ref[z]
                here = tiles[z]
                below = tiles[z - 1] if z else ends[part][0]
                above = tiles[z + 1] if z < planes - 1 else ends[part][1]
                near = below + above
                low = jnp.where(row == 0, low_rows[z : z + 1], pltpu.roll(here, 1, 0))
                high = jnp.where(row == rows - 1, high_rows[z : z + 1], pltpu.roll(here, rows - 1, 0))
                near = near + low + high
                left = jnp.where(lane == 0, 0.0, pltpu.roll(here, 1, 1))
                right = jnp.where(lane == width - 1, 0.0, pltpu.roll(here, width - 1, 1))
                near = near + left + right
                cross = diag_imag * field[1 - part][z]
                applied = diag_real * here - near
                applied = applied - cross if part == 0 else applied + cross
                residual_ref[part, b, z] = source_ref[part, b, z] - applied


def finish(scalars, leaf, source, *others):
    two, sources, planes, rows, width = source.shape
    step = 4
    whole = pl.BlockSpec((two, step, planes, rows, width), lambda i: (0, i, 0, 0, 0))
    return pl.pallas_call(
        final_kernel,
        grid=(sources // step,),
        in_specs=[pl.BlockSpec(memory_space=pltpu.SMEM)] * len(scalars)
        + [whole, whole]
        + [pl.BlockSpec(memory_space=pltpu.VMEM)] * len(others),
        out_specs=[whole, whole],
        out_shape=[jax.ShapeDtypeStruct(source.shape, F32)] * 2,
        compiler_params=pltpu.CompilerParams(vmem_limit_bytes=40 * 2**20),
        cost_estimate=pl.CostEstimate(flops=60000000, bytes_accessed=26000000, transcendentals=0),
        name="finish",
    )(*scalars, leaf, source, *others)


def after(value, *others):
    return lax.optimization_barrier((value, *others))[0]


def local(source, wave_term, leaf_inverse, separator_inverse, restrict_weight, prolong_weight):
    two, sources, planes, rows, width = source.shape
    panel = lax.axis_index("panel")
    front = lax.axis_index("front")
    even_core = front % 2 == 0
    even_panel = panel % 2 == 0
    leaf_matrix = leaf_inverse[:, 0, 0]
    separators = separator_inverse[:, 0, 0]
    place = jnp.stack([even_core.astype(jnp.int32), panel, front])
    vector = (two, sources, width)
    shape = jax.ShapeDtypeStruct

    weights = jnp.stack([restrict_weight, prolong_weight])
    traded_weights = {which: swapped(weights, which) for which in "AB"}
    tables = tuple(traded_weights.values())
    traded_leaf = {
        which: [swapped(after(leaf_matrix[part], *tables), which) for part in range(2)] for which in "AB"
    }
    real_parts, imag_parts = zip(*traded_leaf.values())
    leaf, base_terms, first_plane, last_plane, low_rows, high_rows = leaf_solve(weights, source, leaf_matrix)


    def halves(block):
        return jnp.where(even_core, block[0], block[1])

    def inside(sent, panels, near, far, cross):
        side = moved(sent, within(panels, near, cross))
        opposite = moved(halves(sent), within(panels, far, far))
        back = other_core(jnp.concatenate([side, opposite[None]]))
        return side, opposite, back

    def pair_sum(terms):
        return terms.astype(F32) + other_core(terms).astype(F32)

    every = tuple(range(PANELS))
    pair = after(pair_sum(base_terms), *real_parts)
    side, opposite, back = inside(pair.astype(BF), every, 2, 4, 6)
    near_term = jnp.where(even_core, side, back[:2]).astype(F32)
    far_term = jnp.where(even_core, jnp.stack([opposite, back[2]]), jnp.stack([back[2], opposite])).astype(F32)
    quad = pair + near_term
    slab = pair + side.astype(F32) + back[:2].astype(F32) + far_term
    def by_parity(even_value, odd_value):
        return jnp.where(even_panel, even_value, odd_value)

    by_a = swapped(after(by_parity(last_plane, first_plane), slab), "A")
    by_b = swapped(after(by_parity(first_plane, last_plane), slab), "B")
    plane = shape(first_plane.shape, F32)
    planes_got = whole_call(
        planes_kernel, [plane] * 4, 400000000, "planes", 1,
        place, by_a, by_b, first_plane, last_plane, leaf_matrix, *traded_leaf["A"], *traded_leaf["B"], limit=26,
    )
    base_sums = (pair, quad, slab)
    nothing = jnp.zeros(vector, F32)

    sums = whole_call(
        sums_kernel, [shape((5,) + vector, F32)], 10000000, "edge_sums", 3,
        weights, traded_weights["A"], traded_weights["B"], first_plane, last_plane,
    )[0]

    def gather(level_sums, panels, before):
        own, quad, slab = level_sums
        near = near_part(own, quad, slab, separators)
        return (near, slab, *inside(slab.astype(BF), panels, 8, 16, 24), before, separators)

    def forward_close(level_sums, panels, target, which, before, parcel):
        got = gather(level_sums, panels, before)
        return whole_call(
            functools.partial(forward_kernel, target, which),
            [shape(vector, F32), shape(vector, BF), shape((2,) + vector, BF)], 200000000, "forward", 3,
            place, weights, traded_weights[which], *got, *traded_leaf[which], sums, parcel,
        )

    def backward_close(level_sums, panels, target, keep, which, before, brought):
        got = gather(level_sums, panels, before)
        return whole_call(
            functools.partial(backward_kernel, target, keep, which),
            [shape(vector, F32), shape(vector, BF)], 200000000, "backward", 3,
            place, weights, traded_weights[which], *got, *traded_leaf[which], sums, brought["A"], brought["B"],
        )

    def cross(terms, from_panel, to_panel):
        sent = pair_sum(terms).astype(BF)
        ends = ((from_panel, to_panel),)
        one = moved(sent, across(ends, 0, 2))
        two_ = moved(sent, across(ends, 4, 6))
        back = other_core(jnp.stack([one, two_])).astype(F32)
        one = one.astype(F32)
        own = jnp.where(even_core, one, back[0])
        quad = one + back[0]
        return own, quad, quad + two_.astype(F32) + back[1]

    state, terms, parcel = forward_close(base_sums, every, 0, "A", nothing, jnp.zeros((2,) + vector, BF))
    terms = after(terms, imag_parts[1])
    brought = {}
    for turn, which in enumerate("ABA"):
        target = turn + 1
        sums_now = cross(terms, turn, target)
        if turn > 0:
            brought[which] = swapped(parcel, which)
        total = tuple(a + b for a, b in zip(sums_now, base_sums))
        if turn < 2:
            state, terms, parcel = forward_close(total, (target,), target, "BA"[turn], state, parcel)
        else:
            state, terms = backward_close(total, (target,), target, False, "A", state, brought)
        if turn < 2:
            terms = after(terms, *((by_a, by_b), planes_got)[turn])
    scalars = (place, weights, traded_weights["A"], traded_weights["B"])
    enter, leave, zlow, zhigh = planes_got
    edge = shape(low_rows.shape, BF)
    for turn in range(PANELS - 1):
        from_panel = PANELS - 1 - turn
        target = from_panel - 1
        sums_now = cross(terms, from_panel, target)
        if turn < PANELS - 2:
            state, terms = backward_close(sums_now, (target,), target, True, "BA"[turn], state, brought)
        else:
            got_a, got_b = (swapped(state.astype(BF), which) for which in "AB")
            got = gather((*sums_now[:2], after(sums_now[2], got_a, got_b)), (target,), state)
            state, vectors, near_rows, far_rows = whole_call(
                functools.partial(closing_kernel, target),
                [shape(vector, F32), shape((two, 9, sources, width), F32), edge, edge], 300000000, "closing", 4,
                *scalars, *got, got_a, got_b, brought["A"], brought["B"], parcel,
                leaf_matrix, *traded_leaf["A"], *traded_leaf["B"], low_rows, high_rows, enter, leave, limit=26,
            )
    late = swapped(state, "A")
    near_front = other_core(near_rows)
    chain = [(p * FRONTS + f, p * FRONTS + (f + 1) % FRONTS) for p in range(PANELS) for f in range(1, FRONTS, 2)]
    far_front = moved(far_rows, pairing(chain))
    return tuple(
        finish(
            scalars, leaf, source, wave_term, vectors, late, enter, leave, near_front, far_front, zlow, zhigh
        )
    )


def solution(mesh):
    placed = (
        P(None, None, "panel", "front", None),
        P("panel", "front", None),
        P(None, "panel", "front", None, None),
        P(None, "panel", "front", None, None, None),
        P("panel", "front"),
        P("panel", "front"),
    )
    return jax.shard_map(
        local,
        mesh=mesh,
        in_specs=placed,
        out_specs=(P(None, None, "panel", "front", None), P(None, None, "panel", "front", None)),
        check_vma=False,
    )
```

```python
import functools

import jax
import jax.numpy as jnp
from jax import lax
from jax.experimental import pallas as pl
from jax.experimental.pallas import tpu as pltpu
from jax.sharding import PartitionSpec as P

DAMPING = 0.25
PANELS = 4
FRONTS = 32
AXES = ("panel", "front")
BF = jnp.bfloat16
F32 = jnp.float32
PAIRS = {"A": ((0, 1), (2, 3)), "B": ((1, 2), (0, 3))}


def pairing(swaps):
    target = {}
    for one, two in swaps:
        target[one] = two
        target[two] = one
    for device in range(PANELS * FRONTS):
        target.setdefault(device, device ^ 1)
    return sorted(target.items())


def within(panels, even, odd):
    swaps = []
    for panel in panels:
        for front in range(FRONTS):
            other = front ^ (odd if front % 2 else even)
            swaps.append((panel * FRONTS + front, panel * FRONTS + other))
    return pairing(swaps)


def across(pairs, even, odd):
    swaps = []
    for one, two in pairs:
        for front in range(FRONTS):
            other = front ^ (odd if front % 2 else even)
            swaps.append((one * FRONTS + front, two * FRONTS + other))
    return pairing(swaps)


def moved(block, route):
    return lax.ppermute(block, AXES, route)


def other_core(block):
    return moved(block, pairing(()))


def swapped(block, which):
    return moved(block, across(PAIRS[which], 0, 0))


def product(block, matrix_real, matrix_imag, half):
    by_real = jnp.dot(block, matrix_real, preferred_element_type=F32)
    by_imag = jnp.dot(block, matrix_imag, preferred_element_type=F32)
    return by_real[:half] - by_imag[half:], by_imag[:half] + by_real[half:]


def column(scalars, width):
    row = lax.broadcasted_iota(jnp.int32, (len(scalars), 128), 0)
    tile = jnp.full((len(scalars), 128), scalars[0])
    for i in range(1, len(scalars)):
        tile = jnp.where(row == i, scalars[i], tile)
    return jnp.concatenate([tile] * (width // 128), axis=1)


def dotted(one, two):
    total = one[0] * two[0]
    for a, b in zip(one[1:], two[1:]):
        total = total + a * b
    return total


def entries(ref, kind, plane):
    return [ref[kind, plane, x] for x in range(ref.shape[2])]


def leaf_kernel(weight_ref, source_ref, matrix_ref, leaf_ref, total_ref, first_ref, last_ref, low_ref, high_ref):
    count, planes, rows, width = source_ref.shape[1:]
    flat = count * planes * rows
    real = source_ref[0].reshape(flat, width).astype(BF)
    imag = source_ref[1].reshape(flat, width).astype(BF)
    dot = lambda a, b: jnp.dot(a, b, preferred_element_type=F32)
    out = (
        dot(real, matrix_ref[0]) - dot(imag, matrix_ref[1]),
        dot(real, matrix_ref[1]) + dot(imag, matrix_ref[0]),
    )
    columns = [column(entries(weight_ref, 0, z), width) for z in range(planes)]
    for part in range(2):
        shaped = out[part].reshape(count, planes, rows, width)
        leaf_ref[part] = shaped
        first_ref[part] = shaped[:, 0].astype(BF)
        last_ref[part] = shaped[:, planes - 1].astype(BF)
        low_ref[part] = shaped[:, :, 0]
        high_ref[part] = shaped[:, :, rows - 1]
        total = shaped[:, 0] * columns[0][None]
        for z in range(1, planes):
            total = total + shaped[:, z] * columns[z][None]
        total_ref[part] = jnp.sum(total, axis=1).astype(BF)


def leaf_solve(weights, source, matrix):
    two, sources, planes, rows, width = source.shape
    step = 8
    whole = pl.BlockSpec((two, step, planes, rows, width), lambda i: (0, i, 0, 0, 0))
    plane = pl.BlockSpec((two, step, rows, width), lambda i: (0, i, 0, 0))
    leaf, total, first, last, low, high = pl.pallas_call(
        leaf_kernel,
        grid=(sources // step,),
        in_specs=[
            pl.BlockSpec(memory_space=pltpu.SMEM),
            whole,
            pl.BlockSpec((two, width, width), lambda i: (0, 0, 0)),
        ],
        out_specs=[whole, pl.BlockSpec((two, step, width), lambda i: (0, i, 0)), plane, plane, plane, plane],
        out_shape=[
            pltpu.HBM(source.shape, F32),
            jax.ShapeDtypeStruct((two, sources, width), BF),
            jax.ShapeDtypeStruct((two, sources, rows, width), BF),
            jax.ShapeDtypeStruct((two, sources, rows, width), BF),
            pltpu.HBM((two, sources, planes, width), F32),
            pltpu.HBM((two, sources, planes, width), F32),
        ],
        compiler_params=pltpu.CompilerParams(vmem_limit_bytes=40 * 2**20),
        cost_estimate=pl.CostEstimate(flops=65000000, bytes_accessed=1600000, transcendentals=0),
        name="leaf_solve",
    )(weights, source, matrix)
    return leaf, total, first, last, low, high


def whole_call(kernel, shapes, cost, name, smem, *args, limit=14):
    spaces = [pltpu.SMEM] * smem + [pltpu.VMEM] * (len(args) - smem)
    return pl.pallas_call(
        kernel,
        in_specs=[pl.BlockSpec(memory_space=space) for space in spaces],
        out_specs=[pl.BlockSpec(memory_space=pltpu.VMEM)] * len(shapes),
        out_shape=shapes,
        compiler_params=pltpu.CompilerParams(vmem_limit_bytes=limit * 2**20),
        cost_estimate=pl.CostEstimate(flops=cost, bytes_accessed=cost // 200, transcendentals=0),
        name=name,
    )(*args)


def near_kernel(own_ref, quad_ref, slab_ref, matrix_ref, out_ref, root_ref, held_ref, arrived):
    sources, width = own_ref.shape[1:]
    levels = (own_ref, quad_ref, slab_ref)
    copies = [
        pltpu.make_async_copy(matrix_ref.at[:, level], held_ref.at[level], arrived.at[level])
        for level in range(len(levels))
    ]
    copies.append(pltpu.make_async_copy(matrix_ref.at[:, len(levels)], root_ref, arrived.at[len(levels)]))
    for copy in copies:
        copy.start()
    total = None
    for level, ref in enumerate(levels):
        block = ref[...].reshape(2 * sources, width).astype(BF)
        copies[level].wait()
        got = product(block, held_ref[level, 0], held_ref[level, 1], sources)
        total = got if total is None else (total[0] + got[0], total[1] + got[1])
    out_ref[0] = total[0]
    out_ref[1] = total[1]
    copies[-1].wait()


def near_part(own, quad, slab, separators):
    matrix = (separators.shape[0],) + separators.shape[2:]
    vmem = pl.BlockSpec(memory_space=pltpu.VMEM)
    return pl.pallas_call(
        near_kernel,
        in_specs=[vmem, vmem, vmem, pl.BlockSpec(memory_space=pl.ANY)],
        out_specs=[vmem, vmem],
        out_shape=[jax.ShapeDtypeStruct(own.shape, F32), jax.ShapeDtypeStruct(matrix, BF)],
        scratch_shapes=[pltpu.VMEM((3,) + matrix, BF), pltpu.SemaphoreType.DMA((4,))],
        compiler_params=pltpu.CompilerParams(vmem_limit_bytes=14 * 2**20),
        cost_estimate=pl.CostEstimate(flops=150000000, bytes_accessed=750000, transcendentals=0),
        name="near_part",
    )(own, quad, slab, separators)


def held_kernel(own_ref, quad_ref, slab_ref, matrix_ref, out_ref):
    sources, width = own_ref.shape[1:]
    total = None
    for level, ref in enumerate((own_ref, quad_ref, slab_ref)):
        block = ref[...].reshape(2 * sources, width).astype(BF)
        got = product(block, matrix_ref[0, level], matrix_ref[1, level], sources)
        total = got if total is None else (total[0] + got[0], total[1] + got[1])
    out_ref[0] = total[0]
    out_ref[1] = total[1]


def held_part(own, quad, slab, separators):
    return whole_call(
        held_kernel, [jax.ShapeDtypeStruct(own.shape, F32)], 150000000, "near_part", 0, own, quad, slab, separators
    )[0]


def advanced(target, keep, place_ref, near_ref, slab_ref, side_ref, opposite_ref, back_ref, before_ref, root_ref, state_ref):
    sources, width = near_ref.shape[1:]
    even = place_ref[0] == 1
    active = place_ref[1] == target
    mine = opposite_ref[...].astype(F32)
    other = back_ref[2].astype(F32)
    root = []
    for part in range(2):
        far = jnp.where(even, mine, other) if part == 0 else jnp.where(even, other, mine)
        root.append(slab_ref[part] + side_ref[part].astype(F32) + back_ref[part].astype(F32) + far)
    block = jnp.concatenate(root, axis=0).astype(BF)
    got = product(block, root_ref[0], root_ref[1], sources)
    state = []
    for part in range(2):
        old = before_ref[part]
        new = near_ref[part] + got[part]
        if keep:
            new = new + old
        state.append(jnp.where(active, new, old))
        state_ref[part] = state[part]
    return state, active


def forward_kernel(
    target, which, place_ref, own_ref, traded_ref, near_ref, slab_ref, side_ref, opposite_ref, back_ref, before_ref,
    root_ref, leaf_real_ref, leaf_imag_ref, sums_ref, parcel_ref, state_ref, terms_ref, out_ref,
):
    state, active = advanced(
        target, False, place_ref, near_ref, slab_ref, side_ref, opposite_ref, back_ref, before_ref, root_ref, state_ref
    )
    sources = near_ref.shape[1]
    end = own_ref.shape[1] - 1
    scale = dotted(entries(traded_ref, 0, 0), entries(own_ref, 1, end))
    own_scale = dotted(entries(own_ref, 0, end), entries(own_ref, 1, end))
    rows = []
    for part in range(2):
        here = state[part]
        rows += [sums_ref["AB".index(which), part] + scale * here, here, sums_ref[2, part] + own_scale * here]
    block = jnp.concatenate(rows, axis=0).astype(BF)
    got = product(block, leaf_real_ref[...], leaf_imag_ref[...], 3 * sources)
    for part in range(2):
        terms_ref[part] = got[part][:sources].astype(BF)
        for i in range(2):
            new = got[part][(i + 1) * sources : (i + 2) * sources].astype(BF)
            out_ref[i, part] = jnp.where(active, new, parcel_ref[i, part])


def backward_kernel(
    target, keep, which, place_ref, own_ref, traded_ref, near_ref, slab_ref, side_ref, opposite_ref, back_ref, before_ref,
    root_ref, leaf_real_ref, leaf_imag_ref, sums_ref, by_a_ref, by_b_ref, state_ref, terms_ref,
):
    state, _ = advanced(
        target, keep, place_ref, near_ref, slab_ref, side_ref, opposite_ref, back_ref, before_ref, root_ref, state_ref
    )
    sources = near_ref.shape[1]
    end = own_ref.shape[1] - 1
    even_panel = lax.rem(place_ref[1], 2) == 0
    scale = dotted(entries(traded_ref, 0, end), entries(own_ref, 1, 0))
    rows = []
    for part in range(2):
        echo = jnp.where(even_panel, by_b_ref[1, part], by_a_ref[1, part]).astype(F32)
        rows.append(sums_ref[3 + "AB".index(which), part] + echo + scale * state[part])
    block = jnp.concatenate(rows, axis=0).astype(BF)
    got = product(block, leaf_real_ref[...], leaf_imag_ref[...], sources)
    for part in range(2):
        terms_ref[part] = got[part].astype(BF)


def sums_kernel(own_ref, by_a_ref, by_b_ref, first_ref, last_ref, out_ref):
    width = first_ref.shape[3]
    end = own_ref.shape[1] - 1
    tables = [
        (last_ref, column(entries(by_a_ref, 0, 0), width)),
        (last_ref, column(entries(by_b_ref, 0, 0), width)),
        (last_ref, column(entries(own_ref, 0, end), width)),
        (first_ref, column(entries(by_a_ref, 0, end), width)),
        (first_ref, column(entries(by_b_ref, 0, end), width)),
    ]
    for part in range(2):
        for i, (ref, table) in enumerate(tables):
            out_ref[i, part] = jnp.sum(ref[part].astype(F32) * table[None], axis=1)


def planes_kernel(
    place_ref, by_a_ref, by_b_ref, first_ref, last_ref, own_ref, a_real_ref, a_imag_ref, b_real_ref, b_imag_ref,
    enter_ref, leave_ref, zlow_ref, zhigh_ref,
):
    two, sources, rows, width = first_ref.shape
    flat = sources * rows
    panel = place_ref[1]
    even = lax.rem(panel, 2) == 0
    lower = panel > 0
    upper = panel < PANELS - 1

    def stacked(parts):
        return jnp.concatenate([part.reshape(flat, width) for part in parts], axis=0).astype(BF)

    def times(parts, matrix):
        return [part.reshape(sources, rows, width) for part in product(stacked(parts), matrix[0], matrix[1], flat)]

    below = [jnp.where(even, by_b_ref[part], by_a_ref[part]).astype(F32) for part in range(2)]
    below = [jnp.where(lower, part, 0.0) for part in below]
    above = [jnp.where(even, by_a_ref[part], by_b_ref[part]).astype(F32) for part in range(2)]
    leaf_a, leaf_b = (a_real_ref[...], a_imag_ref[...]), (b_real_ref[...], b_imag_ref[...])
    upper_leaf = [jnp.where(even, leaf_a[part], leaf_b[part]) for part in range(2)]
    lower_leaf = [jnp.where(even, leaf_b[part], leaf_a[part]) for part in range(2)]
    own_leaf = [own_ref[0], own_ref[1]]
    enter = times(below, own_leaf)
    above_enter = times([last_ref[part].astype(F32) for part in range(2)], upper_leaf)
    zhigh = [jnp.where(upper, above[part] + above_enter[part], 0.0) for part in range(2)]
    leave = times(zhigh, own_leaf)
    below_leave = times([first_ref[part].astype(F32) + enter[part] for part in range(2)], lower_leaf)
    for part in range(2):
        enter_ref[part] = enter[part]
        leave_ref[part] = leave[part]
        zhigh_ref[part] = zhigh[part]
        zlow_ref[part] = jnp.where(lower, below[part] + below_leave[part], 0.0)


def neighbour_tables(place_ref, by_a_ref, by_b_ref, end):
    panel = place_ref[1]
    even = lax.rem(panel, 2) == 0
    pick = lambda one, two, there: jnp.where(there, jnp.where(even, one, two), 0.0)
    below = [
        pick(b, a, panel > 0) for a, b in zip(entries(by_a_ref, 1, end), entries(by_b_ref, 1, end))
    ]
    above = [
        pick(a, b, panel < PANELS - 1) for a, b in zip(entries(by_a_ref, 1, 0), entries(by_b_ref, 1, 0))
    ]
    return below, above


def closing_kernel(
    target, place_ref, own_w_ref, a_w_ref, b_w_ref, near_ref, slab_ref, side_ref, opposite_ref, back_ref, before_ref,
    root_ref, got_a_ref, got_b_ref, parcel_a_ref, parcel_b_ref, parcel_ref, own_ref, a_real_ref, a_imag_ref, b_real_ref, b_imag_ref,
    low_ref, high_ref, enter_ref, leave_ref, state_ref, vector_ref, near_rows_ref, far_rows_ref,
):
    here, _ = advanced(
        target, True, place_ref, near_ref, slab_ref, side_ref, opposite_ref, back_ref, before_ref, root_ref, state_ref
    )
    sources, planes, width = low_ref.shape[1:]
    rows = enter_ref.shape[2]
    panel = place_ref[1]
    even_core = place_ref[0] == 1
    even = lax.rem(panel, 2) == 0
    lower = panel > 0
    upper = panel < PANELS - 1
    below_last, above_first = neighbour_tables(place_ref, a_w_ref, b_w_ref, planes - 1)
    own_last = entries(own_w_ref, 1, planes - 1)
    own_leaf = [own_ref[0], own_ref[1]]
    lower_leaf = [jnp.where(even, b, a) for a, b in ((a_real_ref[...], b_real_ref[...]), (a_imag_ref[...], b_imag_ref[...]))]
    entered, above, below, behind = [], [], [], []
    for part in range(2):
        entered.append(jnp.where(lower, jnp.where(even, parcel_b_ref[0, part], parcel_a_ref[0, part]).astype(F32), 0.0))
        above.append(jnp.where(even, got_a_ref[part], got_b_ref[part]).astype(F32))
        below.append(jnp.where(even, got_b_ref[part], got_a_ref[part]).astype(F32))
        behind.append(jnp.where(upper, parcel_ref[0, part].astype(F32), 0.0))
    stacked = lambda one, two: jnp.concatenate([one[0], two[0], one[1], two[1]], axis=0).astype(BF)
    out_up = product(stacked(above, behind), own_leaf[0], own_leaf[1], 2 * sources)
    out_down = product(stacked(here, entered), lower_leaf[0], lower_leaf[1], 2 * sources)
    depth = lax.broadcasted_iota(jnp.int32, (planes, width), 0)
    ends = [column([own_w_ref[1, z, x] for z in range(planes)], width) for x in (0, rows - 1)]
    for part in range(2):
        down = jnp.where(lower, out_down[part], 0.0)
        vectors = [
            here[part], entered[part], above[part], below[part], behind[part],
            out_up[part][:sources], out_up[part][sources:], down[:sources], down[sources:],
        ]
        for i, vector in enumerate(vectors):
            vector_ref[part, i] = vector
        for b in range(sources):
            row = lambda i: vector_ref[part, i, b : b + 1]
            done = []
            for side, ref in ((0, low_ref), (1, high_ref)):
                x = 0 if side == 0 else rows - 1
                enter = enter_ref[part, b, x : x + 1] + below_last[x] * row(1)
                leave = leave_ref[part, b, x : x + 1] + above_first[x] * row(5) + own_last[x] * row(6)
                tile = ref[part, b] + ends[side] * row(0)
                tile = tile + jnp.where(depth == 0, enter, 0.0) + jnp.where(depth == planes - 1, leave, 0.0)
                done.append(tile)
            near_rows_ref[part, b] = jnp.where(even_core, done[1], done[0]).astype(BF)
            far_rows_ref[part, b] = jnp.where(even_core, done[0], done[1]).astype(BF)


def final_kernel(
    place_ref, own_w_ref, a_w_ref, b_w_ref, leaf_ref, source_ref, wave_ref, vector_ref, late_ref, enter_ref, leave_ref,
    near_ref, far_ref, zlow_ref, zhigh_ref, field_ref, residual_ref,
):
    count, planes, rows, width = leaf_ref.shape[1:]
    lane = lax.broadcasted_iota(jnp.int32, (rows, width), 1)
    row = lax.broadcasted_iota(jnp.int32, (rows, width), 0)
    even_core = place_ref[0] == 1
    low_there = place_ref[2] > 0
    high_there = place_ref[2] < FRONTS - 1
    below_last, above_first = (
        column(table, width) for table in neighbour_tables(place_ref, a_w_ref, b_w_ref, planes - 1)
    )
    prolong = [column(entries(own_w_ref, 1, z), width) for z in range(planes)]
    own_last, own_first = prolong[planes - 1], prolong[0]
    even = lax.rem(place_ref[1], 2) == 0
    start = pl.program_id(0) * count
    for b in range(count):
        at = start + b
        field, ends = [], []
        for part in range(2):
            vec = [vector_ref[part, i, pl.ds(at, 1)] for i in range(9)]
            lower = jnp.where(even, vec[3], late_ref[part, pl.ds(at, 1)])
            tiles = []
            for z in range(planes):
                tile = leaf_ref[part, b, z] + prolong[z] * vec[0]
                if z == 0:
                    tile = tile + enter_ref[part, at] + below_last * vec[1]
                if z == planes - 1:
                    tile = tile + leave_ref[part, at] + above_first * vec[5] + own_last * vec[6]
                field_ref[part, b, z] = tile
                tiles.append(tile)
            field.append(tiles)
            below = zlow_ref[part, at] + below_last * (lower + vec[8]) + own_first * vec[7]
            above = zhigh_ref[part, at] + above_first * vec[2] + own_last * vec[4]
            ends.append((below, above))
        for part in range(2):
            tiles = field[part]
            near_rows = near_ref[part, at].astype(F32)
            far_rows = far_ref[part, at].astype(F32)
            low_rows = jnp.where(even_core, jnp.where(low_there, far_rows, 0.0), near_rows)
            high_rows = jnp.where(even_core, near_rows, jnp.where(high_there, far_rows, 0.0))
            for z in range(planes):
                diag_real = 6.0 - wave_ref[z]
                diag_imag = -DAMPING * wave_ref[z]
                here = tiles[z]
                below = tiles[z - 1] if z else ends[part][0]
                above = tiles[z + 1] if z < planes - 1 else ends[part][1]
                near = below + above
                low = jnp.where(row == 0, low_rows[z : z + 1], pltpu.roll(here, 1, 0))
                high = jnp.where(row == rows - 1, high_rows[z : z + 1], pltpu.roll(here, rows - 1, 0))
                near = near + low + high
                left = jnp.where(lane == 0, 0.0, pltpu.roll(here, 1, 1))
                right = jnp.where(lane == width - 1, 0.0, pltpu.roll(here, width - 1, 1))
                near = near + left + right
                cross = diag_imag * field[1 - part][z]
                applied = diag_real * here - near
                applied = applied - cross if part == 0 else applied + cross
                residual_ref[part, b, z] = source_ref[part, b, z] - applied


def finish(scalars, leaf, source, *others):
    two, sources, planes, rows, width = source.shape
    step = 4
    whole = pl.BlockSpec((two, step, planes, rows, width), lambda i: (0, i, 0, 0, 0))
    return pl.pallas_call(
        final_kernel,
        grid=(sources // step,),
        in_specs=[pl.BlockSpec(memory_space=pltpu.SMEM)] * len(scalars)
        + [whole, whole]
        + [pl.BlockSpec(memory_space=pltpu.VMEM)] * len(others),
        out_specs=[whole, whole],
        out_shape=[jax.ShapeDtypeStruct(source.shape, F32)] * 2,
        compiler_params=pltpu.CompilerParams(vmem_limit_bytes=40 * 2**20),
        cost_estimate=pl.CostEstimate(flops=60000000, bytes_accessed=26000000, transcendentals=0),
        name="finish",
    )(*scalars, leaf, source, *others)


def after(value, *others):
    return lax.optimization_barrier((value, *others))[0]


def local(source, wave_term, leaf_inverse, separator_inverse, restrict_weight, prolong_weight):
    source = pltpu.with_memory_space_constraint(source, pltpu.HBM)
    two, sources, planes, rows, width = source.shape
    panel = lax.axis_index("panel")
    front = lax.axis_index("front")
    even_core = front % 2 == 0
    even_panel = panel % 2 == 0
    leaf_matrix = leaf_inverse[:, 0, 0]
    separators = separator_inverse[:, 0, 0]
    root_matrix = separators[:, 3]
    fetched = pltpu.with_memory_space_constraint(separators, pltpu.HBM)
    place = jnp.stack([even_core.astype(jnp.int32), panel, front])
    vector = (two, sources, width)
    shape = jax.ShapeDtypeStruct

    weights = jnp.stack([restrict_weight, prolong_weight])
    traded_weights = {which: swapped(weights, which) for which in "AB"}
    tables = tuple(traded_weights.values())
    traded_leaf = {
        which: [swapped(after(leaf_matrix[part], *tables), which) for part in range(2)] for which in "AB"
    }
    real_parts, imag_parts = zip(*traded_leaf.values())
    leaf, base_terms, first_plane, last_plane, low_rows, high_rows = leaf_solve(weights, source, leaf_matrix)


    def halves(block):
        return jnp.where(even_core, block[0], block[1])

    def inside(sent, panels, near, far, cross):
        side = moved(sent, within(panels, near, cross))
        opposite = moved(halves(sent), within(panels, far, far))
        back = other_core(jnp.concatenate([side, opposite[None]]))
        return side, opposite, back

    def pair_sum(terms):
        return terms.astype(F32) + other_core(terms).astype(F32)

    every = tuple(range(PANELS))
    pair = after(pair_sum(base_terms), *real_parts)
    side, opposite, back = inside(pair.astype(BF), every, 2, 4, 6)
    near_term = jnp.where(even_core, side, back[:2]).astype(F32)
    far_term = jnp.where(even_core, jnp.stack([opposite, back[2]]), jnp.stack([back[2], opposite])).astype(F32)
    quad = pair + near_term
    slab = pair + side.astype(F32) + back[:2].astype(F32) + far_term
    def by_parity(even_value, odd_value):
        return jnp.where(even_panel, even_value, odd_value)

    by_a = swapped(after(by_parity(last_plane, first_plane), slab), "A")
    by_b = swapped(after(by_parity(first_plane, last_plane), slab), "B")
    plane = shape(first_plane.shape, F32)
    planes_got = whole_call(
        planes_kernel, [plane] * 4, 400000000, "planes", 1,
        place, by_a, by_b, first_plane, last_plane, leaf_matrix, *traded_leaf["A"], *traded_leaf["B"], limit=26,
    )
    base_sums = (pair, quad, slab)
    nothing = jnp.zeros(vector, F32)

    sums = whole_call(
        sums_kernel, [shape((5,) + vector, F32)], 10000000, "edge_sums", 3,
        weights, traded_weights["A"], traded_weights["B"], first_plane, last_plane,
    )[0]

    def gather(level_sums, panels, before, first=False):
        own, quad, slab = level_sums
        if first:
            near, root = near_part(own, quad, slab, fetched)
        else:
            near, root = held_part(own, quad, slab, separators), root_matrix
        return (near, slab, *inside(slab.astype(BF), panels, 8, 16, 24), before, root)

    def forward_close(level_sums, panels, target, which, before, parcel):
        got = gather(level_sums, panels, before, target < 2)
        return whole_call(
            functools.partial(forward_kernel, target, which),
            [shape(vector, F32), shape(vector, BF), shape((2,) + vector, BF)], 200000000, "forward", 3,
            place, weights, traded_weights[which], *got, *traded_leaf[which], sums, parcel,
        )

    def backward_close(level_sums, panels, target, keep, which, before, brought):
        got = gather(level_sums, panels, before)
        return whole_call(
            functools.partial(backward_kernel, target, keep, which),
            [shape(vector, F32), shape(vector, BF)], 200000000, "backward", 3,
            place, weights, traded_weights[which], *got, *traded_leaf[which], sums, brought["A"], brought["B"],
        )

    def cross(terms, from_panel, to_panel):
        sent = pair_sum(terms).astype(BF)
        ends = ((from_panel, to_panel),)
        one = moved(sent, across(ends, 0, 2))
        two_ = moved(sent, across(ends, 4, 6))
        back = other_core(jnp.stack([one, two_])).astype(F32)
        one = one.astype(F32)
        own = jnp.where(even_core, one, back[0])
        quad = one + back[0]
        return own, quad, quad + two_.astype(F32) + back[1]

    state, terms, parcel = forward_close(base_sums, every, 0, "A", nothing, jnp.zeros((2,) + vector, BF))
    terms = after(terms, imag_parts[1])
    brought = {}
    for turn, which in enumerate("ABA"):
        target = turn + 1
        sums_now = cross(terms, turn, target)
        if turn > 0:
            brought[which] = swapped(parcel, which)
        total = tuple(a + b for a, b in zip(sums_now, base_sums))
        if turn < 2:
            state, terms, parcel = forward_close(total, (target,), target, "BA"[turn], state, parcel)
        else:
            state, terms = backward_close(total, (target,), target, False, "A", state, brought)
        if turn < 2:
            terms = after(terms, *((by_a, by_b), planes_got)[turn])
    scalars = (place, weights, traded_weights["A"], traded_weights["B"])
    enter, leave, zlow, zhigh = planes_got
    edge = shape(low_rows.shape, BF)
    for turn in range(PANELS - 1):
        from_panel = PANELS - 1 - turn
        target = from_panel - 1
        sums_now = cross(terms, from_panel, target)
        if turn < PANELS - 2:
            state, terms = backward_close(sums_now, (target,), target, True, "BA"[turn], state, brought)
        else:
            got_a, got_b = (swapped(state.astype(BF), which) for which in "AB")
            got = gather((*sums_now[:2], after(sums_now[2], got_a, got_b)), (target,), state)
            state, vectors, near_rows, far_rows = whole_call(
                functools.partial(closing_kernel, target),
                [shape(vector, F32), shape((two, 9, sources, width), F32), edge, edge], 300000000, "closing", 4,
                *scalars, *got, got_a, got_b, brought["A"], brought["B"], parcel,
                leaf_matrix, *traded_leaf["A"], *traded_leaf["B"], low_rows, high_rows, enter, leave, limit=26,
            )
    late = swapped(state, "A")
    near_front = other_core(near_rows)
    chain = [(p * FRONTS + f, p * FRONTS + (f + 1) % FRONTS) for p in range(PANELS) for f in range(1, FRONTS, 2)]
    far_front = moved(far_rows, pairing(chain))
    return tuple(
        finish(
            scalars, leaf, source, wave_term, vectors, late, enter, leave, near_front, far_front, zlow, zhigh
        )
    )


def solution(mesh):
    placed = (
        P(None, None, "panel", "front", None),
        P("panel", "front", None),
        P(None, "panel", "front", None, None),
        P(None, "panel", "front", None, None, None),
        P("panel", "front"),
        P("panel", "front"),
    )
    return jax.shard_map(
        local,
        mesh=mesh,
        in_specs=placed,
        out_specs=(P(None, None, "panel", "front", None), P(None, None, "panel", "front", None)),
        check_vma=False,
    )
```
